32 devices in a mesh: ctx: 16 (over z, y, x), fsdp: 2 (over core).
Axes of the slice: x: 2, y: 2, z: 4, core: 2. Of those that a mesh axis runs over, the one named last changes fastest.
Arguments:
- tokens: bfloat16 [2, 2048, 576], P('fsdp', 'ctx'), may hold values from -6 to 6
- cotangent: bfloat16 [2, 2048, 576], P('fsdp', 'ctx'), may hold values from -6 to 6
- norm_attn: bfloat16 [576], P('fsdp'), may hold values from 0.5 to 1.5
- w_query: bfloat16 [576, 576], P('fsdp'), may hold values from -0.25 to 0.25
- w_key: bfloat16 [576, 192], P('fsdp'), may hold values from -0.25 to 0.25
- w_value: bfloat16 [576, 192], P('fsdp'), may hold values from -0.25 to 0.25
- w_out: bfloat16 [576, 576], P('fsdp'), may hold values from -4 to 4
- norm_ffn: bfloat16 [576], P('fsdp'), may hold values from 0.5 to 1.5
- w_gate: bfloat16 [576, 1536], P('fsdp'), may hold values from -0.25 to 0.25
- w_up: bfloat16 [576, 1536], P('fsdp'), may hold values from -0.25 to 0.25
- w_down: bfloat16 [1536, 576], P('fsdp'), may hold values from -0.15625 to 0.15625
Outputs:
- output: bfloat16 [2, 2048, 576], P('fsdp', 'ctx')
- grad_tokens: float32 [2, 2048, 576], P('fsdp', 'ctx')
- grad_norm_attn: float32 [576], P('fsdp')
- grad_w_query: float32 [576, 576], P('fsdp')
- grad_w_key: float32 [576, 192], P('fsdp')
- grad_w_value: float32 [576, 192], P('fsdp')
- grad_w_out: float32 [576, 576], P('fsdp')
- grad_norm_ffn: float32 [576], P('fsdp')
- grad_w_gate: float32 [576, 1536], P('fsdp')
- grad_w_up: float32 [576, 1536], P('fsdp')
- grad_w_down: float32 [1536, 576], P('fsdp')
The draws below stay inside these ranges and needn't reach their ends.
All inputs are finite; a program needn't handle non-finite values.
Results may differ from the reference program's by a relative error of at most 0.03.
Values may be sent and summed in bfloat16 or wider, within the bound.
A program may use at most 128 MiB of HBM per device.

```python
import math
import jax
import jax.numpy as jnp
from jax import lax

D = 576
HEADS = 9
KV_HEADS = 3
HEAD_DIM = 64
FF = 1536
SEQ = 2048
SEQS = 2


def levels(own_key, dims, cuts, low, largest):
    level = 1.0
    for position, shards_of in cuts:
        heights = jax.random.uniform(jax.random.fold_in(jax.random.fold_in(own_key, 6), position), (shards_of,), jnp.float32, low / len(cuts), largest / len(cuts))
        level = level * jnp.repeat(jnp.exp(heights), dims[position] // shards_of).reshape((-1,) + (1,) * (len(dims) - 1 - position))
    return level


def centred(own_key, shape, spread, most, pieces=(), held_as=jnp.bfloat16):
    values = jax.random.normal(own_key, shape, jnp.float32) * spread
    if len(pieces) > 0:
        values = levels(own_key, shape, pieces, -0.22, 0.18) * values
    return jnp.clip(values, min=-most, max=most).astype(held_as)


def setup_inputs(seed: int = 0) -> dict:
    arg_keys = jax.random.split(jax.random.key(seed), 12)
    return {
        "tokens": centred(arg_keys[0], (SEQS, SEQ, D), 1.0, 6.0, ((0, 2), (1, 16))),
        "cotangent": centred(arg_keys[1], (SEQS, SEQ, D), 1.0, 6.0, ((0, 2), (1, 16))),
        "norm_attn": jnp.clip(1.0 + 0.1 * jax.random.normal(arg_keys[2], (D,), jnp.float32), 0.5, 1.5).astype(jnp.bfloat16),
        "w_query": centred(arg_keys[3], (D, D), D ** -0.5, 0.25, ((0, 2),)),
        "w_key": centred(arg_keys[4], (D, KV_HEADS * HEAD_DIM), D ** -0.5, 0.25, ((0, 2),)),
        "w_value": centred(arg_keys[5], (D, KV_HEADS * HEAD_DIM), D ** -0.5, 0.25, ((0, 2),)),
        "w_out": centred(arg_keys[6], (D, D), 2 ** -0.5, 4.0, ((0, 2),)),
        "norm_ffn": jnp.clip(1.0 + 0.1 * jax.random.normal(arg_keys[7], (D,), jnp.float32), 0.5, 1.5).astype(jnp.bfloat16),
        "w_gate": centred(arg_keys[8], (D, FF), D ** -0.5, 0.25, ((0, 2),)),
        "w_up": centred(arg_keys[9], (D, FF), D ** -0.5, 0.25, ((0, 2),)),
        "w_down": centred(arg_keys[10], (FF, D), FF ** -0.5, 0.15625, ((0, 2),)),
    }


norm_eps = 1e-05
rope_base = 10000.0
masked_score = -1e+30
exact_mode = lax.Precision.HIGHEST

@jax.custom_vjp
def low(v):
    return lax.optimization_barrier(v.astype(jnp.bfloat16)).astype(jnp.float32)

@jax.custom_vjp
def low_back(v):
    return v

def low_keep(v):
    return (low(v), None)

def low_pass(kept, grad):
    return (grad,)

def back_keep(v):
    return (v, None)

def back_low(kept, grad):
    return (low(grad),)
low.defvjp(low_keep, low_pass)
low_back.defvjp(back_keep, back_low)

def matmul_high(left, right):
    return jnp.matmul(left, right, precision=exact_mode)

def rms_norm(values, gain):
    factor = lax.rsqrt(lax.optimization_barrier(jnp.mean(values * values, -1, keepdims=True)) + norm_eps)
    return values * factor * gain

def rope_tables(length, head_width):
    halfway = head_width // 2
    inverse = rope_base ** (-(jnp.arange(halfway, dtype=jnp.float32) * 2.0 / head_width))
    angles = jnp.arange(length, dtype=jnp.float32)[:, None] * inverse[None, :]
    return (jnp.cos(angles)[:, None, :], jnp.sin(angles)[:, None, :])

def rotate(values, cosine_table, sine_table):
    halfway = values.shape[-1] // 2
    former = values[..., :halfway]
    latter = values[..., halfway:]
    return jnp.concatenate([former * cosine_table - latter * sine_table, latter * cosine_table + former * sine_table], -1)

def attend_sequence(query_matrix, keys, values):
    length = query_matrix.shape[0]
    block_rows = math.gcd(length, 512)
    block_count = length // block_rows
    key_places = jnp.arange(length, dtype=jnp.int32)

    def one_block(entry_pair):
        query_block, first_row = entry_pair
        scores = jnp.einsum('bgrd,sgd->grbs', query_block, keys, precision=exact_mode) * HEAD_DIM ** (-0.5)
        scores = low_back(scores)
        query_places = first_row + jnp.arange(block_rows, dtype=jnp.int32)
        allowed = key_places[None, :] <= query_places[:, None]
        scores = jnp.where(allowed, scores, masked_score)
        highest = lax.optimization_barrier(jnp.max(scores, -1, keepdims=True))
        weights = jnp.exp(scores - highest)
        share_portions = low(weights / lax.optimization_barrier(jnp.sum(weights, -1, keepdims=True)))
        return jnp.einsum('grbs,sgd->bgrd', share_portions, values, precision=exact_mode)
    blocks = query_matrix.reshape((block_count, block_rows) + query_matrix.shape[1:])
    starts = (jnp.arange(block_count, dtype=jnp.int32) * block_rows).astype(jnp.int32)
    outcome = lax.map(jax.checkpoint(one_block), (blocks, starts))
    return outcome.reshape(query_matrix.shape)

def forward(inputs, gain_attn, query_w, key_w, value_w, out_w, gain_ffn, gate_w, up_w, down_w):
    seq_count, length, model_width = inputs.shape
    groups = KV_HEADS
    repeat = HEADS // KV_HEADS
    normed = low(rms_norm(inputs, gain_attn))
    query_pre = low_back(matmul_high(normed, query_w))
    key_pre = low_back(matmul_high(normed, key_w))
    value_pre = low_back(matmul_high(normed, value_w))
    cosine_table, sine_table = rope_tables(length, HEAD_DIM)
    query_matrix = low(rotate(query_pre.reshape(seq_count, length, HEADS, HEAD_DIM), cosine_table, sine_table))
    keys = low(rotate(key_pre.reshape(seq_count, length, groups, HEAD_DIM), cosine_table, sine_table))
    values = low(value_pre.reshape(seq_count, length, groups, HEAD_DIM))
    query_matrix = query_matrix.reshape(seq_count, length, groups, repeat, HEAD_DIM)

    def per_sequence(triple):
        return attend_sequence(triple[0], triple[1], triple[2])
    attended = lax.map(per_sequence, (query_matrix, keys, values))
    attn_flat = low(low_back(attended.reshape(seq_count, length, model_width)))
    residual = inputs + low_back(matmul_high(attn_flat, out_w))
    second = low(rms_norm(residual, gain_ffn))
    gate_pre = low_back(matmul_high(second, gate_w))
    upward = low_back(matmul_high(second, up_w))
    hidden = low(jax.nn.silu(gate_pre) * upward)
    return residual + matmul_high(hidden, down_w)

def reference(tokens, cotangent, norm_attn, w_query, w_key, w_value, w_out, norm_ffn, w_gate, w_up, w_down):
    operands = tuple((operand.astype(jnp.float32) for operand in (tokens, norm_attn, w_query, w_key, w_value, w_out, norm_ffn, w_gate, w_up, w_down)))
    result, pullback = jax.vjp(forward, *operands)
    gradients = pullback(cotangent.astype(jnp.float32))
    return (result.astype(jnp.bfloat16), gradients[0], gradients[1], gradients[2], gradients[3], gradients[4], gradients[5], gradients[6], gradients[7], gradients[8], gradients[9])
```

```python
import functools

import jax
import jax.numpy as jnp
from jax import lax
from jax.experimental import pallas as pl
from jax.experimental.pallas import tpu as pltpu
from jax.sharding import PartitionSpec as P

HEADS = 9
KV_HEADS = 3
HEAD_DIM = 64


norm_eps = 1e-05
rope_base = 10000.0
masked_score = -1e30


def rope_tables(first_pos, length, head_width):
    halfway = head_width // 2
    inverse = rope_base ** (-(jnp.arange(halfway, dtype=jnp.float32) * 2.0 / head_width))
    places = (first_pos + jnp.arange(length, dtype=jnp.int32)).astype(jnp.float32)
    angles = places[:, None] * inverse[None, :]
    return (jnp.cos(angles)[:, None, :], jnp.sin(angles)[:, None, :])


def rotate(values, cosine_table, sine_table):
    halfway = values.shape[-1] // 2
    former = values[..., :halfway]
    latter = values[..., halfway:]
    return jnp.concatenate(
        [former * cosine_table - latter * sine_table, latter * cosine_table + former * sine_table],
        -1,
    )


def unrotate(values, cosine_table, sine_table):
    halfway = values.shape[-1] // 2
    former = values[..., :halfway]
    latter = values[..., halfway:]
    return jnp.concatenate(
        [former * cosine_table + latter * sine_table, latter * cosine_table - former * sine_table],
        -1,
    )


def norm_forward(values, gain):
    factor = lax.rsqrt(jnp.mean(values * values, -1, keepdims=True) + norm_eps)
    normed = values * factor
    return (normed * gain, normed, factor)


def norm_backward(incoming, gain, normed, factor):
    scaled = incoming * gain
    back = factor * (scaled - normed * jnp.mean(scaled * normed, -1, keepdims=True))
    return (back, jnp.sum(incoming * normed, 0))


def times_transposed(left, right):
    return lax.dot_general(
        left, right, (((1,), (1,)), ((), ())), preferred_element_type=jnp.float32
    )


def transposed_times(left, right):
    return lax.dot_general(
        left, right, (((0,), (0,)), ((), ())), preferred_element_type=jnp.float32
    )


def block_span(count_rows):
    span_rows = count_rows
    while span_rows > 512 and span_rows % 2 == 0:
        span_rows = span_rows // 2
    return span_rows


def split_pair(block_rows, kv_width, groups):
    rows_here = block_rows.shape[0]
    return (
        block_rows[:, :kv_width].reshape(rows_here, groups, -1),
        block_rows[:, kv_width:].reshape(rows_here, groups, -1),
    )


def reduce_grads(partials):
    own_index = lax.axis_index("fsdp")
    part_count = lax.axis_size("fsdp")
    halves = []
    for partial in partials:
        rows = partial.shape[0] // part_count
        own = lax.dynamic_slice_in_dim(partial, own_index * rows, rows, 0)
        for shift in range(1, part_count):
            other = lax.rem(own_index + shift, part_count)
            sent = lax.dynamic_slice_in_dim(partial, other * rows, rows, 0).astype(jnp.bfloat16)
            moves = [(a, (a + shift) % part_count) for a in range(part_count)]
            own = own + lax.ppermute(sent, "fsdp", moves).astype(jnp.float32)
        halves.append(own.astype(jnp.bfloat16))
    return tuple(h.astype(jnp.float32) for h in lax.psum(tuple(halves), "ctx"))


def heads_stacked(ref, group, repeat):
    first = group * repeat * HEAD_DIM
    return jnp.concatenate(
        [ref[:, first + r * HEAD_DIM : first + (r + 1) * HEAD_DIM] for r in range(repeat)], 0
    )


def heads_beside(transposed, repeat):
    rows = transposed.shape[1] // repeat
    back = transposed.T
    return jnp.concatenate([back[r * rows : (r + 1) * rows] for r in range(repeat)], 1)


def allowed_pairs(first_ref, key_first, keys, rows, repeat):
    key_place = lax.broadcasted_iota(jnp.int32, (keys, repeat * rows), 0)
    query_place = lax.rem(lax.broadcasted_iota(jnp.int32, (keys, repeat * rows), 1), rows)
    return key_place - query_place <= first_ref[0] - key_first


def forward_kernel(first_ref, query_ref, pair_ref, out_ref, log_ref, high_ref, total_ref, sum_ref):
    block, blocks = pl.program_id(0), pl.num_programs(0)
    keys, rows = pair_ref.shape[0], query_ref.shape[0]
    repeat = HEADS // KV_HEADS
    kv_width = KV_HEADS * HEAD_DIM

    @pl.when(block == 0)
    def _():
        high_ref[...] = jnp.full_like(high_ref, masked_score)
        total_ref[...] = jnp.zeros_like(total_ref)
        sum_ref[...] = jnp.zeros_like(sum_ref)

    allowed = allowed_pairs(first_ref, block * keys, keys, rows, repeat)
    for group in range(KV_HEADS):
        stacked = heads_stacked(query_ref, group, repeat)
        k = pair_ref[:, group * HEAD_DIM : (group + 1) * HEAD_DIM]
        v = pair_ref[:, kv_width + group * HEAD_DIM : kv_width + (group + 1) * HEAD_DIM]
        scores = jnp.where(allowed, times_transposed(k, stacked), masked_score)
        old_high = high_ref[group : group + 1, :]
        new_high = jnp.maximum(old_high, jnp.max(scores, 0, keepdims=True))
        weights = jnp.exp(scores - new_high)
        keep = jnp.exp(old_high - new_high)
        total = total_ref[group : group + 1, :] * keep + jnp.sum(weights, 0, keepdims=True)
        summed = sum_ref[group] * keep + transposed_times(v, weights.astype(jnp.bfloat16))
        high_ref[group : group + 1, :] = new_high
        total_ref[group : group + 1, :] = total
        sum_ref[group] = summed

        @pl.when(block == blocks - 1)
        def _():
            log_ref[group : group + 1, :] = new_high + jnp.log(total)
            width = repeat * HEAD_DIM
            out_ref[:, group * width : (group + 1) * width] = heads_beside(summed / total, repeat)


def backward_kernel(
    first_ref, query_ref, grad_ref, out_ref, log_ref, pair_ref, dq_ref, dpair_ref, sum_ref
):
    block, blocks = pl.program_id(0), pl.num_programs(0)
    keys, rows = pair_ref.shape[0], query_ref.shape[0]
    repeat = HEADS // KV_HEADS
    kv_width = KV_HEADS * HEAD_DIM

    @pl.when(block == 0)
    def _():
        sum_ref[...] = jnp.zeros_like(sum_ref)

    allowed = allowed_pairs(first_ref, block * keys, keys, rows, repeat)
    key_parts, value_parts = [], []
    for group in range(KV_HEADS):
        stacked = heads_stacked(query_ref, group, repeat)
        grads = heads_stacked(grad_ref, group, repeat)
        outs = heads_stacked(out_ref, group, repeat)
        inner = jnp.sum((grads.astype(jnp.float32) * outs).T, 0, keepdims=True)
        k = pair_ref[:, group * HEAD_DIM : (group + 1) * HEAD_DIM]
        v = pair_ref[:, kv_width + group * HEAD_DIM : kv_width + (group + 1) * HEAD_DIM]
        scores = times_transposed(k, stacked)
        shares = jnp.where(allowed, jnp.exp(scores - log_ref[group : group + 1, :]), 0.0)
        score_grads = (shares * (times_transposed(v, grads) - inner)).astype(jnp.bfloat16)
        value_parts.append(
            jnp.dot(shares.astype(jnp.bfloat16), grads, preferred_element_type=jnp.float32)
        )
        key_parts.append(jnp.dot(score_grads, stacked, preferred_element_type=jnp.float32))
        summed = sum_ref[group] + transposed_times(k, score_grads)
        sum_ref[group] = summed

        @pl.when(block == blocks - 1)
        def _():
            width = repeat * HEAD_DIM
            dq_ref[:, group * width : (group + 1) * width] = heads_beside(summed, repeat)

    dpair_ref[...] = jnp.concatenate(key_parts + value_parts, 1).astype(dpair_ref.dtype)


def whole_block(shape):
    return pl.BlockSpec(shape, lambda b: (0,) * len(shape))


def attention_forward(first_place, queries, pair):
    rows, width = queries.shape
    keys = block_span(pair.shape[0])
    columns = (HEADS // KV_HEADS) * rows
    return pl.pallas_call(
        forward_kernel,
        grid=(pair.shape[0] // keys,),
        in_specs=[
            pl.BlockSpec(memory_space=pltpu.SMEM),
            whole_block((rows, width)),
            pl.BlockSpec((keys, pair.shape[1]), lambda b: (b, 0)),
        ],
        out_specs=[whole_block((rows, width)), whole_block((KV_HEADS, columns))],
        out_shape=[
            jax.ShapeDtypeStruct((rows, width), jnp.float32),
            jax.ShapeDtypeStruct((KV_HEADS, columns), jnp.float32),
        ],
        scratch_shapes=[
            pltpu.VMEM((KV_HEADS, columns), jnp.float32),
            pltpu.VMEM((KV_HEADS, columns), jnp.float32),
            pltpu.VMEM((KV_HEADS, HEAD_DIM, columns), jnp.float32),
        ],
        compiler_params=pltpu.CompilerParams(vmem_limit_bytes=40 * 1024 * 1024),
    )(first_place, queries, pair)


def attention_backward(first_place, queries, grads, outs, logs, pair):
    rows, width = queries.shape
    keys = block_span(pair.shape[0])
    columns = (HEADS // KV_HEADS) * rows
    return pl.pallas_call(
        backward_kernel,
        grid=(pair.shape[0] // keys,),
        in_specs=[
            pl.BlockSpec(memory_space=pltpu.SMEM),
            whole_block((rows, width)),
            whole_block((rows, width)),
            whole_block((rows, width)),
            whole_block((KV_HEADS, columns)),
            pl.BlockSpec((keys, pair.shape[1]), lambda b: (b, 0)),
        ],
        out_specs=[
            whole_block((rows, width)),
            pl.BlockSpec((keys, pair.shape[1]), lambda b: (b, 0)),
        ],
        out_shape=[
            jax.ShapeDtypeStruct((rows, width), jnp.float32),
            jax.ShapeDtypeStruct(pair.shape, jnp.bfloat16),
        ],
        scratch_shapes=[pltpu.VMEM((KV_HEADS, HEAD_DIM, columns), jnp.float32)],
        compiler_params=pltpu.CompilerParams(vmem_limit_bytes=40 * 1024 * 1024),
    )(first_place, queries, grads, outs, logs, pair)


def body(
    tokens, cotangent, norm_attn, w_query, w_key, w_value, w_out, norm_ffn, w_gate, w_up, w_down
):
    gathered = (
        lax.all_gather(norm_attn, "fsdp", axis=0, tiled=True),
        lax.all_gather(w_query, "fsdp", axis=0, tiled=True),
        lax.all_gather(w_key, "fsdp", axis=0, tiled=True),
        lax.all_gather(w_value, "fsdp", axis=0, tiled=True),
        lax.all_gather(w_out, "fsdp", axis=0, tiled=True),
        lax.all_gather(norm_ffn, "fsdp", axis=0, tiled=True),
        lax.all_gather(w_gate, "fsdp", axis=0, tiled=True),
        lax.all_gather(w_up, "fsdp", axis=0, tiled=True),
        lax.all_gather(w_down, "fsdp", axis=0, tiled=True),
    )
    gain_attn, query_w, key_w, value_w, out_w, gain_ffn, gate_w, up_w, down_w = gathered
    gain_attn = gain_attn.astype(jnp.float32)
    gain_ffn = gain_ffn.astype(jnp.float32)
    local_rows = tokens.shape[1]
    model_width = tokens.shape[2]
    groups = KV_HEADS
    repeat = HEADS // KV_HEADS
    kv_width = KV_HEADS * HEAD_DIM
    score_scale = HEAD_DIM ** (-0.5)
    first_pos = lax.axis_index("ctx") * local_rows
    inputs = tokens[0].astype(jnp.float32)
    grad_output = cotangent[0]
    attn_in, normed_one, factor_one = norm_forward(inputs, gain_attn)
    act_one = attn_in.astype(jnp.bfloat16)
    cosine_table, sine_table = rope_tables(first_pos, local_rows, HEAD_DIM)
    query_pre = jnp.dot(act_one, query_w, preferred_element_type=jnp.float32)
    key_pre = jnp.dot(act_one, key_w, preferred_element_type=jnp.float32)
    value_pre = jnp.dot(act_one, value_w, preferred_element_type=jnp.float32)
    query_matrix = rotate(
        query_pre.reshape(local_rows, HEADS, HEAD_DIM), cosine_table, sine_table
    ).astype(jnp.bfloat16)
    query_matrix = query_matrix.reshape(local_rows, groups, repeat, HEAD_DIM)
    keys_here = rotate(
        key_pre.reshape(local_rows, groups, HEAD_DIM), cosine_table, sine_table
    ).astype(jnp.bfloat16)
    values_here = value_pre.reshape(local_rows, groups, HEAD_DIM).astype(jnp.bfloat16)
    packed = jnp.concatenate(
        [keys_here.reshape(local_rows, kv_width), values_here.reshape(local_rows, kv_width)], 1
    )
    arriving = lax.all_gather(packed, "ctx", axis=0, tiled=True)
    all_rows = arriving.shape[0]
    scaled_queries = (
        query_matrix.reshape(local_rows, model_width) * jnp.bfloat16(score_scale)
    )
    first_place = first_pos.astype(jnp.int32).reshape(1)
    attended, log_totals = attention_forward(first_place, scaled_queries, arriving)
    out_act = attended.reshape(local_rows, model_width).astype(jnp.bfloat16)
    residual = inputs + jnp.dot(out_act, out_w, preferred_element_type=jnp.float32)
    ffn_in, normed_two, factor_two = norm_forward(residual, gain_ffn)
    act_two = ffn_in.astype(jnp.bfloat16)
    gate_pre = jnp.dot(act_two, gate_w, preferred_element_type=jnp.float32)
    upward = jnp.dot(act_two, up_w, preferred_element_type=jnp.float32)
    silu_gate = jax.nn.silu(gate_pre)
    hidden = (silu_gate * upward).astype(jnp.bfloat16)
    result = (residual + jnp.dot(hidden, down_w, preferred_element_type=jnp.float32)).astype(
        jnp.bfloat16
    )
    grad_hidden = times_transposed(grad_output, down_w)
    grad_down_w = transposed_times(hidden, grad_output)
    sigmoid_gate = jax.nn.sigmoid(gate_pre)
    grad_gate = (
        grad_hidden * upward * sigmoid_gate * (1.0 + gate_pre * (1.0 - sigmoid_gate))
    ).astype(jnp.bfloat16)
    grad_upward = (grad_hidden * silu_gate).astype(jnp.bfloat16)
    grad_gate_w = transposed_times(act_two, grad_gate)
    grad_up_w = transposed_times(act_two, grad_upward)
    grad_act_two = times_transposed(grad_gate, gate_w) + times_transposed(grad_upward, up_w)
    back_two, grad_gain_ffn = norm_backward(grad_act_two, gain_ffn, normed_two, factor_two)
    grad_residual = grad_output.astype(jnp.float32) + back_two
    grad_attn = grad_residual.astype(jnp.bfloat16)
    grad_out_w = transposed_times(out_act, grad_attn)
    reduce_early = reduce_grads((grad_gate_w, grad_up_w, grad_down_w, grad_out_w))
    grad_flat = times_transposed(grad_attn, out_w).astype(jnp.bfloat16)
    grad_queries, partial_pair = attention_backward(
        first_place, scaled_queries, grad_flat, attended, log_totals, arriving
    )
    grad_queries = grad_queries * score_scale
    summed_pair = lax.psum_scatter(partial_pair, "ctx", scatter_dimension=0, tiled=True)
    grad_keys, grad_values = split_pair(summed_pair.astype(jnp.float32), kv_width, groups)
    grad_query_pre = (
        unrotate(grad_queries.reshape(local_rows, HEADS, HEAD_DIM), cosine_table, sine_table)
        .reshape(local_rows, model_width)
        .astype(jnp.bfloat16)
    )
    grad_key_pre = (
        unrotate(grad_keys, cosine_table, sine_table)
        .reshape(local_rows, kv_width)
        .astype(jnp.bfloat16)
    )
    grad_value_pre = grad_values.reshape(local_rows, kv_width).astype(jnp.bfloat16)
    grad_query_w = transposed_times(act_one, grad_query_pre)
    grad_key_w = transposed_times(act_one, grad_key_pre)
    grad_value_w = transposed_times(act_one, grad_value_pre)
    grad_act_one = (
        times_transposed(grad_query_pre, query_w)
        + times_transposed(grad_key_pre, key_w)
        + times_transposed(grad_value_pre, value_w)
    )
    back_one, grad_gain_attn = norm_backward(grad_act_one, gain_attn, normed_one, factor_one)
    grad_input = grad_residual + back_one
    reduce_early, late_grads = lax.optimization_barrier(
        (
            reduce_early,
            (grad_query_w, grad_key_w, grad_value_w, grad_gain_attn, grad_gain_ffn),
        )
    )
    shards = reduce_early + reduce_grads(late_grads)
    return (
        result[None],
        grad_input[None],
        shards[7],
        shards[4],
        shards[5],
        shards[6],
        shards[3],
        shards[8],
        shards[0],
        shards[1],
        shards[2],
    )


def solution(mesh):
    placed = (
        P("fsdp", "ctx", None),
        P("fsdp", "ctx", None),
        P("fsdp"),
        P("fsdp", None),
        P("fsdp", None),
        P("fsdp", None),
        P("fsdp", None),
        P("fsdp"),
        P("fsdp", None),
        P("fsdp", None),
        P("fsdp", None),
    )
    return jax.shard_map(
        body,
        mesh=mesh,
        in_specs=placed,
        out_specs=(
            P("fsdp", "ctx", None),
            P("fsdp", "ctx", None),
            P("fsdp"),
            P("fsdp", None),
            P("fsdp", None),
            P("fsdp", None),
            P("fsdp", None),
            P("fsdp"),
            P("fsdp", None),
            P("fsdp", None),
            P("fsdp", None),
        ),
        check_vma=False,
    )
```

```python
import functools

import jax
import jax.numpy as jnp
from jax import lax
from jax.experimental import pallas as pl
from jax.experimental.pallas import tpu as pltpu
from jax.sharding import PartitionSpec as P

HEADS = 9
KV_HEADS = 3
HEAD_DIM = 64


norm_eps = 1e-05
rope_base = 10000.0
masked_score = -1e30


def rope_tables(first_pos, length, head_width):
    halfway = head_width // 2
    inverse = rope_base ** (-(jnp.arange(halfway, dtype=jnp.float32) * 2.0 / head_width))
    places = (first_pos + jnp.arange(length, dtype=jnp.int32)).astype(jnp.float32)
    angles = places[:, None] * inverse[None, :]
    return (jnp.cos(angles)[:, None, :], jnp.sin(angles)[:, None, :])


def rotate(values, cosine_table, sine_table):
    halfway = values.shape[-1] // 2
    former = values[..., :halfway]
    latter = values[..., halfway:]
    return jnp.concatenate(
        [former * cosine_table - latter * sine_table, latter * cosine_table + former * sine_table],
        -1,
    )


def unrotate(values, cosine_table, sine_table):
    halfway = values.shape[-1] // 2
    former = values[..., :halfway]
    latter = values[..., halfway:]
    return jnp.concatenate(
        [former * cosine_table + latter * sine_table, latter * cosine_table - former * sine_table],
        -1,
    )


def norm_forward(values, gain):
    factor = lax.rsqrt(jnp.mean(values * values, -1, keepdims=True) + norm_eps)
    normed = values * factor
    return (normed * gain, normed, factor)


def norm_backward(incoming, gain, normed, factor):
    scaled = incoming * gain
    back = factor * (scaled - normed * jnp.mean(scaled * normed, -1, keepdims=True))
    return (back, jnp.sum(incoming * normed, 0))


def times_transposed(left, right):
    return lax.dot_general(
        left, right, (((1,), (1,)), ((), ())), preferred_element_type=jnp.float32
    )


def transposed_times(left, right):
    return lax.dot_general(
        left, right, (((0,), (0,)), ((), ())), preferred_element_type=jnp.float32
    )


def block_span(count_rows):
    span_rows = count_rows
    while span_rows > 512 and span_rows % 2 == 0:
        span_rows = span_rows // 2
    return span_rows


def bit_count(devices):
    return devices.bit_length() - 1


def gather_orders(devices):
    order = list(range(bit_count(devices)))[::-1]
    return (order, order[:-2] + order[-2:][::-1])


def reduce_orders(devices):
    order = list(range(bit_count(devices)))
    return (order, order[:2][::-1] + order[2:], order[2:] + order[:2])


def swap(values, bit):
    count = lax.axis_size("ctx")
    return lax.ppermute(values, "ctx", [(i, i ^ (1 << bit)) for i in range(count)])


def own_bit(bit):
    return lax.rem(lax.axis_index("ctx") // (1 << bit), 2)


def gather_tree(block, order):
    held = block
    for bit in order:
        held = jnp.concatenate([held, swap(held, bit)], 0)
    return held


def scatter_tree(slots, order):
    held = slots.astype(jnp.float32)
    for bit in order[::-1]:
        half = held.shape[0] // 2
        held = held[:half] + swap(held[half:].astype(jnp.bfloat16), bit).astype(jnp.float32)
    return held


def middle_swapped(slots, order):
    if len(order) < 2:
        return slots
    part = slots.shape[0] // 4
    return jnp.concatenate(
        [slots[:part], slots[2 * part : 3 * part], slots[part : 2 * part], slots[3 * part :]], 0
    )


def slot_places(rows, order):
    slots = jnp.arange(1 << len(order), dtype=jnp.int32)
    flips = jnp.zeros_like(slots)
    for place, bit in enumerate(order):
        flips = flips + ((slots >> place) & 1) * (1 << bit)
    owners = flips ^ lax.axis_index("ctx").astype(jnp.int32)
    return (owners[:, None] * rows + jnp.arange(rows, dtype=jnp.int32)[None, :]).reshape(-1, 1)


def core_half(partial):
    own_index = lax.axis_index("fsdp")
    part_count = lax.axis_size("fsdp")
    rows = partial.shape[0] // part_count
    own = lax.dynamic_slice_in_dim(partial, own_index * rows, rows, 0)
    for shift in range(1, part_count):
        other = lax.rem(own_index + shift, part_count)
        sent = lax.dynamic_slice_in_dim(partial, other * rows, rows, 0).astype(jnp.bfloat16)
        moves = [(a, (a + shift) % part_count) for a in range(part_count)]
        own = own + lax.ppermute(sent, "fsdp", moves).astype(jnp.float32)
    return own


def reduce_tree(partial, order):
    held = partial
    path = []
    for bit in order:
        axis = 0 if held.shape[0] % 16 == 0 else 1
        half = held.shape[axis] // 2
        mine = own_bit(bit)
        kept = lax.dynamic_slice_in_dim(held, mine * half, half, axis)
        sent = lax.dynamic_slice_in_dim(held, (1 - mine) * half, half, axis)
        held = kept + swap(sent.astype(jnp.bfloat16), bit).astype(jnp.float32)
        path.append((bit, axis))
    held = held.astype(jnp.bfloat16)
    for bit, axis in path[::-1]:
        other = swap(held, bit)
        held = jnp.where(
            own_bit(bit) == 0,
            jnp.concatenate([held, other], axis),
            jnp.concatenate([other, held], axis),
        )
    return held.astype(jnp.float32)


def sum_tree(partial, order):
    held = partial
    for bit in order:
        held = held + swap(held, bit)
    count = lax.axis_size("fsdp")
    parts = held
    for shift in range(1, count):
        moves = [(a, (a + shift) % count) for a in range(count)]
        parts = parts + lax.ppermute(held, "fsdp", moves)
    held = parts
    return held


def heads_stacked(ref, group, repeat):
    first = group * repeat * HEAD_DIM
    return jnp.concatenate(
        [ref[:, first + r * HEAD_DIM : first + (r + 1) * HEAD_DIM] for r in range(repeat)], 0
    )


def heads_beside(transposed, repeat):
    rows = transposed.shape[1] // repeat
    back = transposed.T
    return jnp.concatenate([back[r * rows : (r + 1) * rows] for r in range(repeat)], 1)


def allowed_pairs(first_ref, place_ref, rows, repeat):
    query_place = lax.rem(lax.broadcasted_iota(jnp.int32, (1, repeat * rows), 1), rows)
    return place_ref[...] <= query_place + first_ref[0]


def forward_kernel(
    first_ref,
    place_ref,
    query_ref,
    key_ref,
    value_ref,
    out_ref,
    log_ref,
    high_ref,
    total_ref,
    sum_ref,
):
    block, blocks = pl.program_id(0), pl.num_programs(0)
    rows = query_ref.shape[0]
    repeat = HEADS // KV_HEADS

    @pl.when(block == 0)
    def _():
        high_ref[...] = jnp.full_like(high_ref, masked_score)
        total_ref[...] = jnp.zeros_like(total_ref)
        sum_ref[...] = jnp.zeros_like(sum_ref)

    allowed = allowed_pairs(first_ref, place_ref, rows, repeat)
    for group in range(KV_HEADS):
        stacked = heads_stacked(query_ref, group, repeat)
        k = key_ref[:, group * HEAD_DIM : (group + 1) * HEAD_DIM]
        v = value_ref[:, group * HEAD_DIM : (group + 1) * HEAD_DIM]
        scores = jnp.where(allowed, times_transposed(k, stacked), masked_score)
        old_high = high_ref[group : group + 1, :]
        new_high = jnp.maximum(old_high, jnp.max(scores, 0, keepdims=True))
        weights = jnp.exp(scores - new_high)
        keep = jnp.exp(old_high - new_high)
        total = total_ref[group : group + 1, :] * keep + jnp.sum(weights, 0, keepdims=True)
        summed = sum_ref[group] * keep + transposed_times(v, weights.astype(jnp.bfloat16))
        high_ref[group : group + 1, :] = new_high
        total_ref[group : group + 1, :] = total
        sum_ref[group] = summed

        @pl.when(block == blocks - 1)
        def _():
            log_ref[group : group + 1, :] = new_high + jnp.log(total)
            width = repeat * HEAD_DIM
            out_ref[:, group * width : (group + 1) * width] = heads_beside(summed / total, repeat)


def backward_kernel(
    first_ref,
    place_ref,
    query_ref,
    grad_ref,
    out_ref,
    log_ref,
    key_ref,
    value_ref,
    dq_ref,
    dkey_ref,
    dvalue_ref,
    sum_ref,
):
    block, blocks = pl.program_id(0), pl.num_programs(0)
    rows = query_ref.shape[0]
    repeat = HEADS // KV_HEADS

    @pl.when(block == 0)
    def _():
        sum_ref[...] = jnp.zeros_like(sum_ref)

    allowed = allowed_pairs(first_ref, place_ref, rows, repeat)
    key_parts, value_parts = [], []
    for group in range(KV_HEADS):
        stacked = heads_stacked(query_ref, group, repeat)
        grads = heads_stacked(grad_ref, group, repeat)
        outs = heads_stacked(out_ref, group, repeat)
        inner = jnp.sum((grads.astype(jnp.float32) * outs).T, 0, keepdims=True)
        k = key_ref[:, group * HEAD_DIM : (group + 1) * HEAD_DIM]
        v = value_ref[:, group * HEAD_DIM : (group + 1) * HEAD_DIM]
        scores = times_transposed(k, stacked)
        shares = jnp.where(allowed, jnp.exp(scores - log_ref[group : group + 1, :]), 0.0)
        score_grads = (shares * (times_transposed(v, grads) - inner)).astype(jnp.bfloat16)
        value_parts.append(
            jnp.dot(shares.astype(jnp.bfloat16), grads, preferred_element_type=jnp.float32)
        )
        key_parts.append(jnp.dot(score_grads, stacked, preferred_element_type=jnp.float32))
        summed = sum_ref[group] + transposed_times(k, score_grads)
        sum_ref[group] = summed

        @pl.when(block == blocks - 1)
        def _():
            width = repeat * HEAD_DIM
            dq_ref[:, group * width : (group + 1) * width] = heads_beside(summed, repeat)

    dkey_ref[...] = jnp.concatenate(key_parts, 1).astype(dkey_ref.dtype)
    dvalue_ref[...] = jnp.concatenate(value_parts, 1).astype(dvalue_ref.dtype)


def whole_block(shape):
    return pl.BlockSpec(shape, lambda b: (0,) * len(shape))


def attention_forward(first_place, places, queries, all_keys, all_values):
    rows, width = queries.shape
    keys = block_span(all_keys.shape[0])
    kv_block = pl.BlockSpec((keys, all_keys.shape[1]), lambda b: (b, 0))
    columns = (HEADS // KV_HEADS) * rows
    return pl.pallas_call(
        forward_kernel,
        grid=(all_keys.shape[0] // keys,),
        in_specs=[
            pl.BlockSpec(memory_space=pltpu.SMEM),
            pl.BlockSpec((keys, 1), lambda b: (b, 0)),
            whole_block((rows, width)),
            kv_block,
            kv_block,
        ],
        out_specs=[whole_block((rows, width)), whole_block((KV_HEADS, columns))],
        out_shape=[
            jax.ShapeDtypeStruct((rows, width), jnp.float32),
            jax.ShapeDtypeStruct((KV_HEADS, columns), jnp.float32),
        ],
        scratch_shapes=[
            pltpu.VMEM((KV_HEADS, columns), jnp.float32),
            pltpu.VMEM((KV_HEADS, columns), jnp.float32),
            pltpu.VMEM((KV_HEADS, HEAD_DIM, columns), jnp.float32),
        ],
        compiler_params=pltpu.CompilerParams(vmem_limit_bytes=40 * 1024 * 1024),
    )(first_place, places, queries, all_keys, all_values)


def attention_backward(first_place, places, queries, grads, outs, logs, all_keys, all_values):
    rows, width = queries.shape
    keys = block_span(all_keys.shape[0])
    kv_block = pl.BlockSpec((keys, all_keys.shape[1]), lambda b: (b, 0))
    columns = (HEADS // KV_HEADS) * rows
    return pl.pallas_call(
        backward_kernel,
        grid=(all_keys.shape[0] // keys,),
        in_specs=[
            pl.BlockSpec(memory_space=pltpu.SMEM),
            pl.BlockSpec((keys, 1), lambda b: (b, 0)),
            whole_block((rows, width)),
            whole_block((rows, width)),
            whole_block((rows, width)),
            whole_block((KV_HEADS, columns)),
            kv_block,
            kv_block,
        ],
        out_specs=[
            whole_block((rows, width)),
            kv_block,
            kv_block,
        ],
        out_shape=[
            jax.ShapeDtypeStruct((rows, width), jnp.float32),
            jax.ShapeDtypeStruct(all_keys.shape, jnp.bfloat16),
            jax.ShapeDtypeStruct(all_keys.shape, jnp.bfloat16),
        ],
        scratch_shapes=[pltpu.VMEM((KV_HEADS, HEAD_DIM, columns), jnp.float32)],
        compiler_params=pltpu.CompilerParams(vmem_limit_bytes=40 * 1024 * 1024),
    )(first_place, places, queries, grads, outs, logs, all_keys, all_values)


def body(
    tokens, cotangent, norm_attn, w_query, w_key, w_value, w_out, norm_ffn, w_gate, w_up, w_down
):
    gathered = (
        lax.all_gather(norm_attn, "fsdp", axis=0, tiled=True),
        lax.all_gather(w_query, "fsdp", axis=0, tiled=True),
        lax.all_gather(w_key, "fsdp", axis=0, tiled=True),
        lax.all_gather(w_value, "fsdp", axis=0, tiled=True),
        lax.all_gather(w_out, "fsdp", axis=0, tiled=True),
        lax.all_gather(norm_ffn, "fsdp", axis=0, tiled=True),
        lax.all_gather(w_gate, "fsdp", axis=0, tiled=True),
        lax.all_gather(w_up, "fsdp", axis=0, tiled=True),
        lax.all_gather(w_down, "fsdp", axis=0, tiled=True),
    )
    gain_attn, query_w, key_w, value_w, out_w, gain_ffn, gate_w, up_w, down_w = gathered
    gain_attn = gain_attn.astype(jnp.float32)
    gain_ffn = gain_ffn.astype(jnp.float32)
    local_rows = tokens.shape[1]
    model_width = tokens.shape[2]
    groups = KV_HEADS
    repeat = HEADS // KV_HEADS
    kv_width = KV_HEADS * HEAD_DIM
    score_scale = HEAD_DIM ** (-0.5)
    first_pos = lax.axis_index("ctx") * local_rows
    inputs = tokens[0].astype(jnp.float32)
    grad_output = cotangent[0]
    attn_in, normed_one, factor_one = norm_forward(inputs, gain_attn)
    act_one = attn_in.astype(jnp.bfloat16)
    cosine_table, sine_table = rope_tables(first_pos, local_rows, HEAD_DIM)
    query_pre = jnp.dot(act_one, query_w, preferred_element_type=jnp.float32)
    key_pre = jnp.dot(act_one, key_w, preferred_element_type=jnp.float32)
    value_pre = jnp.dot(act_one, value_w, preferred_element_type=jnp.float32)
    query_matrix = rotate(
        query_pre.reshape(local_rows, HEADS, HEAD_DIM), cosine_table, sine_table
    ).astype(jnp.bfloat16)
    query_matrix = query_matrix.reshape(local_rows, groups, repeat, HEAD_DIM)
    keys_here = rotate(
        key_pre.reshape(local_rows, groups, HEAD_DIM), cosine_table, sine_table
    ).astype(jnp.bfloat16)
    values_here = value_pre.reshape(local_rows, groups, HEAD_DIM).astype(jnp.bfloat16)
    key_order, value_order = gather_orders(lax.axis_size("ctx"))
    all_keys = gather_tree(keys_here.reshape(local_rows, kv_width), key_order)
    all_values = middle_swapped(
        gather_tree(values_here.reshape(local_rows, kv_width), value_order), value_order
    )
    places = slot_places(local_rows, key_order)
    scaled_queries = (
        query_matrix.reshape(local_rows, model_width) * jnp.bfloat16(score_scale)
    )
    first_place = first_pos.astype(jnp.int32).reshape(1)
    attended, log_totals = attention_forward(
        first_place, places, scaled_queries, all_keys, all_values
    )
    out_act = attended.reshape(local_rows, model_width).astype(jnp.bfloat16)
    residual = inputs + jnp.dot(out_act, out_w, preferred_element_type=jnp.float32)
    ffn_in, normed_two, factor_two = norm_forward(residual, gain_ffn)
    act_two = ffn_in.astype(jnp.bfloat16)
    gate_pre = jnp.dot(act_two, gate_w, preferred_element_type=jnp.float32)
    upward = jnp.dot(act_two, up_w, preferred_element_type=jnp.float32)
    silu_gate = jax.nn.silu(gate_pre)
    hidden = (silu_gate * upward).astype(jnp.bfloat16)
    result = (residual + jnp.dot(hidden, down_w, preferred_element_type=jnp.float32)).astype(
        jnp.bfloat16
    )
    grad_hidden = times_transposed(grad_output, down_w)
    grad_down_w = transposed_times(hidden, grad_output)
    sigmoid_gate = jax.nn.sigmoid(gate_pre)
    grad_gate = (
        grad_hidden * upward * sigmoid_gate * (1.0 + gate_pre * (1.0 - sigmoid_gate))
    ).astype(jnp.bfloat16)
    grad_upward = (grad_hidden * silu_gate).astype(jnp.bfloat16)
    grad_gate_w = transposed_times(act_two, grad_gate)
    grad_up_w = transposed_times(act_two, grad_upward)
    grad_act_two = times_transposed(grad_gate, gate_w) + times_transposed(grad_upward, up_w)
    back_two, grad_gain_ffn = norm_backward(grad_act_two, gain_ffn, normed_two, factor_two)
    grad_residual = grad_output.astype(jnp.float32) + back_two
    grad_attn = grad_residual.astype(jnp.bfloat16)
    grad_out_w = transposed_times(out_act, grad_attn)
    first_order, second_order, third_order = reduce_orders(lax.axis_size("ctx"))
    shard_gate = reduce_tree(core_half(grad_gate_w), first_order)
    shard_up = reduce_tree(core_half(grad_up_w), second_order)
    shard_down = reduce_tree(core_half(grad_down_w), third_order)
    grad_flat = times_transposed(grad_attn, out_w).astype(jnp.bfloat16)
    grad_queries, partial_keys, partial_values = attention_backward(
        first_place, places, scaled_queries, grad_flat, attended, log_totals, all_keys, all_values
    )
    grad_queries = grad_queries * score_scale
    grad_keys = scatter_tree(partial_keys, key_order).reshape(local_rows, groups, HEAD_DIM)
    grad_values = scatter_tree(middle_swapped(partial_values, value_order), value_order)
    grad_query_pre = (
        unrotate(grad_queries.reshape(local_rows, HEADS, HEAD_DIM), cosine_table, sine_table)
        .reshape(local_rows, model_width)
        .astype(jnp.bfloat16)
    )
    grad_key_pre = (
        unrotate(grad_keys, cosine_table, sine_table)
        .reshape(local_rows, kv_width)
        .astype(jnp.bfloat16)
    )
    grad_value_pre = grad_values.reshape(local_rows, kv_width).astype(jnp.bfloat16)
    grad_query_w = transposed_times(act_one, grad_query_pre)
    grad_key_w = transposed_times(act_one, grad_key_pre)
    grad_value_w = transposed_times(act_one, grad_value_pre)
    grad_act_one = (
        times_transposed(grad_query_pre, query_w)
        + times_transposed(grad_key_pre, key_w)
        + times_transposed(grad_value_pre, value_w)
    )
    back_one, grad_gain_attn = norm_backward(grad_act_one, gain_attn, normed_one, factor_one)
    grad_input = grad_residual + back_one
    shard_one = reduce_tree(
        core_half(jnp.concatenate([grad_out_w, grad_key_w], 1)), first_order
    )
    shard_two = reduce_tree(
        core_half(jnp.concatenate([grad_query_w, grad_value_w], 1)), second_order
    )
    shard_out, shard_key = shard_one[:, :model_width], shard_one[:, model_width:]
    shard_query, shard_value = shard_two[:, :model_width], shard_two[:, model_width:]
    gains = sum_tree(jnp.stack([grad_gain_attn, grad_gain_ffn]), first_order)
    shard_gains = lax.dynamic_slice_in_dim(
        gains, lax.axis_index("fsdp") * norm_attn.shape[0], norm_attn.shape[0], 1
    )
    return (
        result[None],
        grad_input[None],
        shard_gains[0],
        shard_query,
        shard_key,
        shard_value,
        shard_out,
        shard_gains[1],
        shard_gate,
        shard_up,
        shard_down,
    )


def solution(mesh):
    placed = (
        P("fsdp", "ctx", None),
        P("fsdp", "ctx", None),
        P("fsdp"),
        P("fsdp", None),
        P("fsdp", None),
        P("fsdp", None),
        P("fsdp", None),
        P("fsdp"),
        P("fsdp", None),
        P("fsdp", None),
        P("fsdp", None),
    )
    return jax.shard_map(
        body,
        mesh=mesh,
        in_specs=placed,
        out_specs=(
            P("fsdp", "ctx", None),
            P("fsdp", "ctx", None),
            P("fsdp"),
            P("fsdp", None),
            P("fsdp", None),
            P("fsdp", None),
            P("fsdp", None),
            P("fsdp"),
            P("fsdp", None),
            P("fsdp", None),
            P("fsdp", None),
        ),
        check_vma=False,
    )
```

```python
import functools

import jax
import jax.numpy as jnp
from jax import lax
from jax.experimental import pallas as pl
from jax.experimental.pallas import tpu as pltpu
from jax.sharding import PartitionSpec as P

HEADS = 9
KV_HEADS = 3
HEAD_DIM = 64


norm_eps = 1e-05
rope_base = 10000.0
masked_score = -1e30


def rope_tables(first_pos, length, head_width):
    halfway = head_width // 2
    inverse = rope_base ** (-(jnp.arange(halfway, dtype=jnp.float32) * 2.0 / head_width))
    places = (first_pos + jnp.arange(length, dtype=jnp.int32)).astype(jnp.float32)
    angles = places[:, None] * inverse[None, :]
    return (jnp.cos(angles)[:, None, :], jnp.sin(angles)[:, None, :])


def rotate(values, cosine_table, sine_table):
    halfway = values.shape[-1] // 2
    former = values[..., :halfway]
    latter = values[..., halfway:]
    return jnp.concatenate(
        [former * cosine_table - latter * sine_table, latter * cosine_table + former * sine_table],
        -1,
    )


def unrotate(values, cosine_table, sine_table):
    halfway = values.shape[-1] // 2
    former = values[..., :halfway]
    latter = values[..., halfway:]
    return jnp.concatenate(
        [former * cosine_table + latter * sine_table, latter * cosine_table - former * sine_table],
        -1,
    )


def norm_forward(values, gain):
    factor = lax.rsqrt(jnp.mean(values * values, -1, keepdims=True) + norm_eps)
    normed = values * factor
    return (normed * gain, normed, factor)


def norm_backward(incoming, gain, normed, factor):
    scaled = incoming * gain
    back = factor * (scaled - normed * jnp.mean(scaled * normed, -1, keepdims=True))
    return (back, jnp.sum(incoming * normed, 0))


def times_transposed(left, right):
    return lax.dot_general(
        left, right, (((1,), (1,)), ((), ())), preferred_element_type=jnp.float32
    )


def transposed_times(left, right):
    return lax.dot_general(
        left, right, (((0,), (0,)), ((), ())), preferred_element_type=jnp.float32
    )


def block_span(count_rows):
    span_rows = count_rows
    while span_rows > 512 and span_rows % 2 == 0:
        span_rows = span_rows // 2
    return span_rows


def bit_count(devices):
    return devices.bit_length() - 1


def gather_orders(devices):
    order = list(range(bit_count(devices)))[::-1]
    return (order, order[:-2] + order[-2:][::-1])


def reduce_orders(devices):
    order = list(range(bit_count(devices)))
    return (order, order[:2][::-1] + order[2:], order[2:] + order[:2])


def swap(values, bit):
    count = lax.axis_size("ctx")
    return lax.ppermute(values, "ctx", [(i, i ^ (1 << bit)) for i in range(count)])


def own_bit(bit):
    return lax.rem(lax.axis_index("ctx") // (1 << bit), 2)


def gather_tree(block, order):
    held = block
    for bit in order:
        held = jnp.concatenate([held, swap(held, bit)], 0)
    return held


def lockstep(*trees):
    results = [None] * len(trees)
    running = list(range(len(trees)))
    sent = [None] * len(trees)
    while running:
        held = {}
        for place in list(running):
            try:
                held[place] = trees[place].send(sent[place])
            except StopIteration as done:
                results[place] = done.value
                running.remove(place)
        if held:
            tied = lax.optimization_barrier(tuple(held.values()))
            for place, value in zip(held, tied):
                sent[place] = value
    return results


def scatter_tree(slots, order):
    held = slots.astype(jnp.float32)
    for bit in order[::-1]:
        half = held.shape[0] // 2
        held = held[:half] + swap(held[half:].astype(jnp.bfloat16), bit).astype(jnp.float32)
        held = yield held
    return held


def middle_swapped(slots, order):
    if len(order) < 2:
        return slots
    part = slots.shape[0] // 4
    return jnp.concatenate(
        [slots[:part], slots[2 * part : 3 * part], slots[part : 2 * part], slots[3 * part :]], 0
    )


def slot_places(rows, order):
    slots = jnp.arange(1 << len(order), dtype=jnp.int32)
    flips = jnp.zeros_like(slots)
    for place, bit in enumerate(order):
        flips = flips + ((slots >> place) & 1) * (1 << bit)
    owners = flips ^ lax.axis_index("ctx").astype(jnp.int32)
    return (owners[:, None] * rows + jnp.arange(rows, dtype=jnp.int32)[None, :]).reshape(-1, 1)


def core_half(partial):
    own_index = lax.axis_index("fsdp")
    part_count = lax.axis_size("fsdp")
    rows = partial.shape[0] // part_count
    own = lax.dynamic_slice_in_dim(partial, own_index * rows, rows, 0)
    for shift in range(1, part_count):
        other = lax.rem(own_index + shift, part_count)
        sent = lax.dynamic_slice_in_dim(partial, other * rows, rows, 0).astype(jnp.bfloat16)
        moves = [(a, (a + shift) % part_count) for a in range(part_count)]
        own = own + lax.ppermute(sent, "fsdp", moves).astype(jnp.float32)
    return own


def halve_tree(partial, order):
    held = partial
    for bit, axis in tree_path(partial.shape, order):
        half = held.shape[axis] // 2
        mine = own_bit(bit)
        kept = lax.dynamic_slice_in_dim(held, mine * half, half, axis)
        sent = lax.dynamic_slice_in_dim(held, (1 - mine) * half, half, axis)
        held = kept + swap(sent.astype(jnp.bfloat16), bit).astype(jnp.float32)
        held = yield held
    return held.astype(jnp.bfloat16)


def double_tree(piece, shape, order):
    held = piece
    for bit, axis in tree_path(shape, order)[::-1]:
        other = swap(held, bit)
        held = jnp.where(
            own_bit(bit) == 0,
            jnp.concatenate([held, other], axis),
            jnp.concatenate([other, held], axis),
        )
        held = yield held
    return held.astype(jnp.float32)


def tree_path(shape, order):
    rows, path = shape[0], []
    for bit in order:
        axis = 0 if rows % 16 == 0 else 1
        rows = rows // 2 if axis == 0 else rows
        path.append((bit, axis))
    return path


def core_gather(block, axis):
    if lax.axis_size("fsdp") != 2:
        return lax.all_gather(block, "fsdp", axis=axis, tiled=True)
    other = lax.ppermute(block, "fsdp", [(0, 1), (1, 0)])
    return jnp.where(
        lax.axis_index("fsdp") == 0,
        jnp.concatenate([block, other], axis),
        jnp.concatenate([other, block], axis),
    )


def sum_tree(partial, order):
    held = partial
    for bit in order:
        held = held + swap(held, bit)
        held = yield held
    count = lax.axis_size("fsdp")
    parts = held
    for shift in range(1, count):
        moves = [(a, (a + shift) % count) for a in range(count)]
        parts = parts + lax.ppermute(held, "fsdp", moves)
    held = parts
    return held


def heads_stacked(ref, group, repeat):
    first = group * repeat * HEAD_DIM
    return jnp.concatenate(
        [ref[:, first + r * HEAD_DIM : first + (r + 1) * HEAD_DIM] for r in range(repeat)], 0
    )


def heads_beside(transposed, repeat):
    rows = transposed.shape[1] // repeat
    back = transposed.T
    return jnp.concatenate([back[r * rows : (r + 1) * rows] for r in range(repeat)], 1)


def allowed_pairs(first_ref, place_ref, rows, repeat):
    query_place = lax.rem(lax.broadcasted_iota(jnp.int32, (1, repeat * rows), 1), rows)
    return place_ref[...] <= query_place + first_ref[0]


def forward_kernel(
    first_ref,
    place_ref,
    query_ref,
    key_ref,
    value_ref,
    out_ref,
    log_ref,
    high_ref,
    total_ref,
    sum_ref,
):
    block, blocks = pl.program_id(0), pl.num_programs(0)
    rows = query_ref.shape[0]
    repeat = HEADS // KV_HEADS

    @pl.when(block == 0)
    def _():
        high_ref[...] = jnp.full_like(high_ref, masked_score)
        total_ref[...] = jnp.zeros_like(total_ref)
        sum_ref[...] = jnp.zeros_like(sum_ref)

    allowed = allowed_pairs(first_ref, place_ref, rows, repeat)
    for group in range(KV_HEADS):
        stacked = heads_stacked(query_ref, group, repeat)
        k = key_ref[:, group * HEAD_DIM : (group + 1) * HEAD_DIM]
        v = value_ref[:, group * HEAD_DIM : (group + 1) * HEAD_DIM]
        scores = jnp.where(allowed, times_transposed(k, stacked), masked_score)
        old_high = high_ref[group : group + 1, :]
        new_high = jnp.maximum(old_high, jnp.max(scores, 0, keepdims=True))
        weights = jnp.exp(scores - new_high)
        keep = jnp.exp(old_high - new_high)
        total = total_ref[group : group + 1, :] * keep + jnp.sum(weights, 0, keepdims=True)
        summed = sum_ref[group] * keep + transposed_times(v, weights.astype(jnp.bfloat16))
        high_ref[group : group + 1, :] = new_high
        total_ref[group : group + 1, :] = total
        sum_ref[group] = summed

        @pl.when(block == blocks - 1)
        def _():
            log_ref[group : group + 1, :] = new_high + jnp.log(total)
            width = repeat * HEAD_DIM
            out_ref[:, group * width : (group + 1) * width] = heads_beside(summed / total, repeat)


def backward_kernel(
    first_ref,
    place_ref,
    query_ref,
    grad_ref,
    out_ref,
    log_ref,
    key_ref,
    value_ref,
    dq_ref,
    dkey_ref,
    dvalue_ref,
    sum_ref,
):
    block, blocks = pl.program_id(0), pl.num_programs(0)
    rows = query_ref.shape[0]
    repeat = HEADS // KV_HEADS

    @pl.when(block == 0)
    def _():
        sum_ref[...] = jnp.zeros_like(sum_ref)

    allowed = allowed_pairs(first_ref, place_ref, rows, repeat)
    key_parts, value_parts = [], []
    for group in range(KV_HEADS):
        stacked = heads_stacked(query_ref, group, repeat)
        grads = heads_stacked(grad_ref, group, repeat)
        outs = heads_stacked(out_ref, group, repeat)
        inner = jnp.sum((grads.astype(jnp.float32) * outs).T, 0, keepdims=True)
        k = key_ref[:, group * HEAD_DIM : (group + 1) * HEAD_DIM]
        v = value_ref[:, group * HEAD_DIM : (group + 1) * HEAD_DIM]
        scores = times_transposed(k, stacked)
        shares = jnp.where(allowed, jnp.exp(scores - log_ref[group : group + 1, :]), 0.0)
        score_grads = (shares * (times_transposed(v, grads) - inner)).astype(jnp.bfloat16)
        value_parts.append(
            jnp.dot(shares.astype(jnp.bfloat16), grads, preferred_element_type=jnp.float32)
        )
        key_parts.append(jnp.dot(score_grads, stacked, preferred_element_type=jnp.float32))
        summed = sum_ref[group] + transposed_times(k, score_grads)
        sum_ref[group] = summed

        @pl.when(block == blocks - 1)
        def _():
            width = repeat * HEAD_DIM
            dq_ref[:, group * width : (group + 1) * width] = heads_beside(summed, repeat)

    dkey_ref[...] = jnp.concatenate(key_parts, 1).astype(dkey_ref.dtype)
    dvalue_ref[...] = jnp.concatenate(value_parts, 1).astype(dvalue_ref.dtype)


def whole_block(shape):
    return pl.BlockSpec(shape, lambda b: (0,) * len(shape))


def attention_forward(first_place, places, queries, all_keys, all_values):
    rows, width = queries.shape
    keys = block_span(all_keys.shape[0])
    kv_block = pl.BlockSpec((keys, all_keys.shape[1]), lambda b: (b, 0))
    columns = (HEADS // KV_HEADS) * rows
    return pl.pallas_call(
        forward_kernel,
        grid=(all_keys.shape[0] // keys,),
        in_specs=[
            pl.BlockSpec(memory_space=pltpu.SMEM),
            pl.BlockSpec((keys, 1), lambda b: (b, 0)),
            whole_block((rows, width)),
            kv_block,
            kv_block,
        ],
        out_specs=[whole_block((rows, width)), whole_block((KV_HEADS, columns))],
        out_shape=[
            jax.ShapeDtypeStruct((rows, width), jnp.float32),
            jax.ShapeDtypeStruct((KV_HEADS, columns), jnp.float32),
        ],
        scratch_shapes=[
            pltpu.VMEM((KV_HEADS, columns), jnp.float32),
            pltpu.VMEM((KV_HEADS, columns), jnp.float32),
            pltpu.VMEM((KV_HEADS, HEAD_DIM, columns), jnp.float32),
        ],
        compiler_params=pltpu.CompilerParams(vmem_limit_bytes=40 * 1024 * 1024),
        cost_estimate=pl.CostEstimate(
            flops=40 * all_keys.shape[0] * columns * HEAD_DIM,
            bytes_accessed=16 * 1024 * all_keys.shape[0],
            transcendentals=KV_HEADS * all_keys.shape[0] * columns,
        ),
    )(first_place, places, queries, all_keys, all_values)


def attention_backward(first_place, places, queries, grads, outs, logs, all_keys, all_values):
    rows, width = queries.shape
    keys = block_span(all_keys.shape[0])
    kv_block = pl.BlockSpec((keys, all_keys.shape[1]), lambda b: (b, 0))
    columns = (HEADS // KV_HEADS) * rows
    return pl.pallas_call(
        backward_kernel,
        grid=(all_keys.shape[0] // keys,),
        in_specs=[
            pl.BlockSpec(memory_space=pltpu.SMEM),
            pl.BlockSpec((keys, 1), lambda b: (b, 0)),
            whole_block((rows, width)),
            whole_block((rows, width)),
            whole_block((rows, width)),
            whole_block((KV_HEADS, columns)),
            kv_block,
            kv_block,
        ],
        out_specs=[
            whole_block((rows, width)),
            kv_block,
            kv_block,
        ],
        out_shape=[
            jax.ShapeDtypeStruct((rows, width), jnp.float32),
            jax.ShapeDtypeStruct(all_keys.shape, jnp.bfloat16),
            jax.ShapeDtypeStruct(all_keys.shape, jnp.bfloat16),
        ],
        scratch_shapes=[pltpu.VMEM((KV_HEADS, HEAD_DIM, columns), jnp.float32)],
        compiler_params=pltpu.CompilerParams(vmem_limit_bytes=40 * 1024 * 1024),
        cost_estimate=pl.CostEstimate(
            flops=40 * all_keys.shape[0] * columns * HEAD_DIM,
            bytes_accessed=16 * 1024 * all_keys.shape[0],
            transcendentals=KV_HEADS * all_keys.shape[0] * columns,
        ),
    )(first_place, places, queries, grads, outs, logs, all_keys, all_values)


def body(
    tokens, cotangent, norm_attn, w_query, w_key, w_value, w_out, norm_ffn, w_gate, w_up, w_down
):
    model_width = tokens.shape[2]
    kv_width = KV_HEADS * HEAD_DIM
    gains = core_gather(jnp.stack([norm_attn, norm_ffn]), 1)
    gain_attn, gain_ffn = gains[0], gains[1]
    joined_w = core_gather(jnp.concatenate([w_query, w_key, w_value], 1), 0)
    out_w = core_gather(w_out, 0)
    gate_w = lax.all_gather(w_gate, "fsdp", axis=0, tiled=True)
    up_w = lax.all_gather(w_up, "fsdp", axis=0, tiled=True)
    down_w = lax.all_gather(w_down, "fsdp", axis=0, tiled=True)
    gain_attn = gain_attn.astype(jnp.float32)
    gain_ffn = gain_ffn.astype(jnp.float32)
    local_rows = tokens.shape[1]
    groups = KV_HEADS
    repeat = HEADS // KV_HEADS
    kv_width = KV_HEADS * HEAD_DIM
    score_scale = HEAD_DIM ** (-0.5)
    first_pos = lax.axis_index("ctx") * local_rows
    inputs = tokens[0].astype(jnp.float32)
    grad_output = cotangent[0]
    attn_in, normed_one, factor_one = norm_forward(inputs, gain_attn)
    act_one = attn_in.astype(jnp.bfloat16)
    cosine_table, sine_table = rope_tables(first_pos, local_rows, HEAD_DIM)
    joined_pre = jnp.dot(act_one, joined_w, preferred_element_type=jnp.float32)
    query_pre = joined_pre[:, :model_width]
    key_pre = joined_pre[:, model_width : model_width + kv_width]
    value_pre = joined_pre[:, model_width + kv_width :]
    query_matrix = rotate(
        query_pre.reshape(local_rows, HEADS, HEAD_DIM), cosine_table, sine_table
    ).astype(jnp.bfloat16)
    query_matrix = query_matrix.reshape(local_rows, groups, repeat, HEAD_DIM)
    keys_here = rotate(
        key_pre.reshape(local_rows, groups, HEAD_DIM), cosine_table, sine_table
    ).astype(jnp.bfloat16)
    values_here = value_pre.reshape(local_rows, groups, HEAD_DIM).astype(jnp.bfloat16)
    key_order, value_order = gather_orders(lax.axis_size("ctx"))
    all_keys = gather_tree(keys_here.reshape(local_rows, kv_width), key_order)
    all_values = middle_swapped(
        gather_tree(values_here.reshape(local_rows, kv_width), value_order), value_order
    )
    places = slot_places(local_rows, key_order)
    scaled_queries = (
        query_matrix.reshape(local_rows, model_width) * jnp.bfloat16(score_scale)
    )
    first_place = first_pos.astype(jnp.int32).reshape(1)
    attended, log_totals = attention_forward(
        first_place, places, scaled_queries, all_keys, all_values
    )
    out_act = attended.reshape(local_rows, model_width).astype(jnp.bfloat16)
    residual = inputs + jnp.dot(out_act, out_w, preferred_element_type=jnp.float32)
    ffn_in, normed_two, factor_two = norm_forward(residual, gain_ffn)
    act_two = ffn_in.astype(jnp.bfloat16)
    gate_pre = jnp.dot(act_two, gate_w, preferred_element_type=jnp.float32)
    upward = jnp.dot(act_two, up_w, preferred_element_type=jnp.float32)
    silu_gate = jax.nn.silu(gate_pre)
    hidden = (silu_gate * upward).astype(jnp.bfloat16)
    result = (residual + jnp.dot(hidden, down_w, preferred_element_type=jnp.float32)).astype(
        jnp.bfloat16
    )
    grad_hidden = times_transposed(grad_output, down_w)
    grad_down_w = transposed_times(hidden, grad_output)
    sigmoid_gate = jax.nn.sigmoid(gate_pre)
    grad_gate = (
        grad_hidden * upward * sigmoid_gate * (1.0 + gate_pre * (1.0 - sigmoid_gate))
    ).astype(jnp.bfloat16)
    grad_upward = (grad_hidden * silu_gate).astype(jnp.bfloat16)
    grad_gate_w = transposed_times(act_two, grad_gate)
    grad_up_w = transposed_times(act_two, grad_upward)
    grad_act_two = times_transposed(grad_gate, gate_w) + times_transposed(grad_upward, up_w)
    back_two, grad_gain_ffn = norm_backward(grad_act_two, gain_ffn, normed_two, factor_two)
    grad_residual = grad_output.astype(jnp.float32) + back_two
    grad_attn = grad_residual.astype(jnp.bfloat16)
    grad_out_w = transposed_times(out_act, grad_attn)
    first_order, second_order, third_order = reduce_orders(lax.axis_size("ctx"))
    half_gate, half_up, half_down = (
        core_half(grad_gate_w),
        core_half(grad_up_w),
        core_half(grad_down_w),
    )
    grad_flat = times_transposed(grad_attn, out_w).astype(jnp.bfloat16)
    half_gate, half_up, half_down, grad_flat = lax.optimization_barrier(
        (half_gate, half_up, half_down, grad_flat)
    )
    grad_queries, partial_keys, partial_values = attention_backward(
        first_place, places, scaled_queries, grad_flat, attended, log_totals, all_keys, all_values
    )
    grad_queries = grad_queries * score_scale
    grad_keys, grad_values, piece_gate, piece_up, piece_down = lockstep(
        scatter_tree(partial_keys, key_order),
        scatter_tree(middle_swapped(partial_values, value_order), value_order),
        halve_tree(half_gate, first_order),
        halve_tree(half_up, second_order),
        halve_tree(half_down, third_order),
    )
    grad_keys = grad_keys.reshape(local_rows, groups, HEAD_DIM)
    grad_query_pre = (
        unrotate(grad_queries.reshape(local_rows, HEADS, HEAD_DIM), cosine_table, sine_table)
        .reshape(local_rows, model_width)
        .astype(jnp.bfloat16)
    )
    grad_key_pre = (
        unrotate(grad_keys, cosine_table, sine_table)
        .reshape(local_rows, kv_width)
        .astype(jnp.bfloat16)
    )
    grad_value_pre = grad_values.reshape(local_rows, kv_width).astype(jnp.bfloat16)
    grad_query_w = transposed_times(act_one, grad_query_pre)
    grad_key_w = transposed_times(act_one, grad_key_pre)
    grad_value_w = transposed_times(act_one, grad_value_pre)
    grad_joined_pre = jnp.concatenate([grad_query_pre, grad_key_pre, grad_value_pre], 1)
    grad_act_one = times_transposed(grad_joined_pre, joined_w)
    back_one, grad_gain_attn = norm_backward(grad_act_one, gain_attn, normed_one, factor_one)
    grad_input = grad_residual + back_one
    half_one = core_half(jnp.concatenate([grad_out_w, grad_key_w], 1))
    half_two = core_half(jnp.concatenate([grad_query_w, grad_value_w], 1))
    piece_one, piece_two, gains_sum, shard_gate, shard_up, shard_down = lockstep(
        halve_tree(half_one, first_order),
        halve_tree(half_two, second_order),
        sum_tree(jnp.stack([grad_gain_attn, grad_gain_ffn]), first_order),
        double_tree(piece_gate, half_gate.shape, first_order),
        double_tree(piece_up, half_up.shape, second_order),
        double_tree(piece_down, half_down.shape, third_order),
    )
    shard_one, shard_two = lockstep(
        double_tree(piece_one, half_one.shape, first_order),
        double_tree(piece_two, half_two.shape, second_order),
    )
    shard_out, shard_key = shard_one[:, :model_width], shard_one[:, model_width:]
    shard_query, shard_value = shard_two[:, :model_width], shard_two[:, model_width:]
    shard_gains = lax.dynamic_slice_in_dim(
        gains_sum, lax.axis_index("fsdp") * norm_attn.shape[0], norm_attn.shape[0], 1
    )
    return (
        result[None],
        grad_input[None],
        shard_gains[0],
        shard_query,
        shard_key,
        shard_value,
        shard_out,
        shard_gains[1],
        shard_gate,
        shard_up,
        shard_down,
    )


def solution(mesh):
    placed = (
        P("fsdp", "ctx", None),
        P("fsdp", "ctx", None),
        P("fsdp"),
        P("fsdp", None),
        P("fsdp", None),
        P("fsdp", None),
        P("fsdp", None),
        P("fsdp"),
        P("fsdp", None),
        P("fsdp", None),
        P("fsdp", None),
    )
    return jax.shard_map(
        body,
        mesh=mesh,
        in_specs=placed,
        out_specs=(
            P("fsdp", "ctx", None),
            P("fsdp", "ctx", None),
            P("fsdp"),
            P("fsdp", None),
            P("fsdp", None),
            P("fsdp", None),
            P("fsdp", None),
            P("fsdp"),
            P("fsdp", None),
            P("fsdp", None),
            P("fsdp", None),
        ),
        check_vma=False,
    )
```

```python
import functools

import jax
import jax.numpy as jnp
from jax import lax
from jax.experimental import pallas as pl
from jax.experimental.pallas import tpu as pltpu
from jax.sharding import PartitionSpec as P

HEADS = 9
KV_HEADS = 3
HEAD_DIM = 64


norm_eps = 1e-05
rope_base = 10000.0
masked_score = -1e30


def rope_tables(first_pos, length, head_width):
    halfway = head_width // 2
    inverse = rope_base ** (-(jnp.arange(halfway, dtype=jnp.float32) * 2.0 / head_width))
    places = (first_pos + jnp.arange(length, dtype=jnp.int32)).astype(jnp.float32)
    angles = places[:, None] * inverse[None, :]
    return (jnp.cos(angles)[:, None, :], jnp.sin(angles)[:, None, :])


def rotate(values, cosine_table, sine_table):
    halfway = values.shape[-1] // 2
    former = values[..., :halfway]
    latter = values[..., halfway:]
    return jnp.concatenate(
        [former * cosine_table - latter * sine_table, latter * cosine_table + former * sine_table],
        -1,
    )


def unrotate(values, cosine_table, sine_table):
    halfway = values.shape[-1] // 2
    former = values[..., :halfway]
    latter = values[..., halfway:]
    return jnp.concatenate(
        [former * cosine_table + latter * sine_table, latter * cosine_table - former * sine_table],
        -1,
    )


def norm_forward(values, gain):
    factor = lax.rsqrt(jnp.mean(values * values, -1, keepdims=True) + norm_eps)
    normed = values * factor
    return (normed * gain, normed, factor)


def norm_backward(incoming, gain, normed, factor):
    scaled = incoming * gain
    back = factor * (scaled - normed * jnp.mean(scaled * normed, -1, keepdims=True))
    return (back, jnp.sum(incoming * normed, 0))


def times_transposed(left, right):
    return lax.dot_general(
        left, right, (((1,), (1,)), ((), ())), preferred_element_type=jnp.float32
    )


def transposed_times(left, right):
    return lax.dot_general(
        left, right, (((0,), (0,)), ((), ())), preferred_element_type=jnp.float32
    )


def block_span(count_rows):
    span_rows = count_rows
    while span_rows > 512 and span_rows % 2 == 0:
        span_rows = span_rows // 2
    return span_rows


def bit_count(devices):
    return devices.bit_length() - 1


def gather_orders(devices):
    order = list(range(bit_count(devices)))[::-1]
    return (order, order[:-2] + order[-2:][::-1])


def reduce_orders(devices):
    order = list(range(bit_count(devices)))
    return (order, order[:2][::-1] + order[2:], order[2:] + order[:2])


def swap(values, bit):
    count = lax.axis_size("ctx")
    return lax.ppermute(values, "ctx", [(i, i ^ (1 << bit)) for i in range(count)])


def own_bit(bit):
    return lax.rem(lax.axis_index("ctx") // (1 << bit), 2)


def gather_tree(block, order):
    held = block
    for bit in order:
        held = jnp.concatenate([held, swap(held, bit)], 0)
    return held


def scatter_tree(slots, order):
    held = slots.astype(jnp.float32)
    for bit in order[::-1]:
        half = held.shape[0] // 2
        held = held[:half] + swap(held[half:].astype(jnp.bfloat16), bit).astype(jnp.float32)
    return held


def middle_swapped(slots, order):
    if len(order) < 2:
        return slots
    part = slots.shape[0] // 4
    return jnp.concatenate(
        [slots[:part], slots[2 * part : 3 * part], slots[part : 2 * part], slots[3 * part :]], 0
    )


def slot_places(rows, order):
    slots = jnp.arange(1 << len(order), dtype=jnp.int32)
    flips = jnp.zeros_like(slots)
    for place, bit in enumerate(order):
        flips = flips + ((slots >> place) & 1) * (1 << bit)
    owners = flips ^ lax.axis_index("ctx").astype(jnp.int32)
    return (owners[:, None] * rows + jnp.arange(rows, dtype=jnp.int32)[None, :]).reshape(-1, 1)


def core_half(*partials):
    own_index = lax.axis_index("fsdp")
    part_count = lax.axis_size("fsdp")
    rows = partials[0].shape[0] // part_count

    def rows_of(index):
        return [lax.dynamic_slice_in_dim(p, index * rows, rows, 0) for p in partials]

    own = jnp.concatenate(rows_of(own_index), 1)
    for shift in range(1, part_count):
        other = lax.rem(own_index + shift, part_count)
        sent = jnp.concatenate([p.astype(jnp.bfloat16) for p in rows_of(other)], 1)
        moves = [(a, (a + shift) % part_count) for a in range(part_count)]
        own = own + lax.ppermute(sent, "fsdp", moves).astype(jnp.float32)
    return own


def halve_tree(partial, order):
    held = partial
    for bit, axis in tree_path(partial.shape, order):
        half = held.shape[axis] // 2
        mine = own_bit(bit)
        kept = lax.dynamic_slice_in_dim(held, mine * half, half, axis)
        sent = lax.dynamic_slice_in_dim(held, (1 - mine) * half, half, axis)
        held = kept + swap(sent.astype(jnp.bfloat16), bit).astype(jnp.float32)
    return held.astype(jnp.bfloat16)


def double_tree(piece, shape, order):
    held = piece
    for bit, axis in tree_path(shape, order)[::-1]:
        other = swap(held, bit)
        held = jnp.where(
            own_bit(bit) == 0,
            jnp.concatenate([held, other], axis),
            jnp.concatenate([other, held], axis),
        )
    return held.astype(jnp.float32)


def tree_path(shape, order):
    rows, path = shape[0], []
    for bit in order:
        axis = 0 if rows % 16 == 0 else 1
        rows = rows // 2 if axis == 0 else rows
        path.append((bit, axis))
    return path


def core_gather(block, axis):
    if lax.axis_size("fsdp") != 2:
        return lax.all_gather(block, "fsdp", axis=axis, tiled=True)
    other = lax.ppermute(block, "fsdp", [(0, 1), (1, 0)])
    return jnp.where(
        lax.axis_index("fsdp") == 0,
        jnp.concatenate([block, other], axis),
        jnp.concatenate([other, block], axis),
    )


def reduce_tree(partial, order):
    return double_tree(halve_tree(partial, order), partial.shape, order)


def heads_stacked(ref, group, repeat):
    first = group * repeat * HEAD_DIM
    return jnp.concatenate(
        [ref[:, first + r * HEAD_DIM : first + (r + 1) * HEAD_DIM] for r in range(repeat)], 0
    )


def heads_beside(transposed, repeat):
    rows = transposed.shape[1] // repeat
    back = transposed.T
    return jnp.concatenate([back[r * rows : (r + 1) * rows] for r in range(repeat)], 1)


def allowed_pairs(first_ref, place_ref, rows, repeat):
    query_place = lax.rem(lax.broadcasted_iota(jnp.int32, (1, repeat * rows), 1), rows)
    return place_ref[...] <= query_place + first_ref[0]


def forward_kernel(
    first_ref,
    place_ref,
    query_ref,
    key_ref,
    value_ref,
    out_ref,
    log_ref,
    high_ref,
    total_ref,
    sum_ref,
):
    block, blocks = pl.program_id(0), pl.num_programs(0)
    rows = query_ref.shape[0]
    repeat = HEADS // KV_HEADS

    @pl.when(block == 0)
    def _():
        high_ref[...] = jnp.full_like(high_ref, masked_score)
        total_ref[...] = jnp.zeros_like(total_ref)
        sum_ref[...] = jnp.zeros_like(sum_ref)

    allowed = allowed_pairs(first_ref, place_ref, rows, repeat)
    for group in range(KV_HEADS):
        stacked = heads_stacked(query_ref, group, repeat)
        k = key_ref[:, group * HEAD_DIM : (group + 1) * HEAD_DIM]
        v = value_ref[:, group * HEAD_DIM : (group + 1) * HEAD_DIM]
        scores = jnp.where(allowed, times_transposed(k, stacked), masked_score)
        old_high = high_ref[group : group + 1, :]
        new_high = jnp.maximum(old_high, jnp.max(scores, 0, keepdims=True))
        weights = jnp.exp(scores - new_high)
        keep = jnp.exp(old_high - new_high)
        total = total_ref[group : group + 1, :] * keep + jnp.sum(weights, 0, keepdims=True)
        summed = sum_ref[group] * keep + transposed_times(v, weights.astype(jnp.bfloat16))
        high_ref[group : group + 1, :] = new_high
        total_ref[group : group + 1, :] = total
        sum_ref[group] = summed

        @pl.when(block == blocks - 1)
        def _():
            log_ref[group : group + 1, :] = new_high + jnp.log(total)
            width = repeat * HEAD_DIM
            out_ref[:, group * width : (group + 1) * width] = heads_beside(summed / total, repeat)


def backward_kernel(
    first_ref,
    place_ref,
    query_ref,
    grad_ref,
    out_ref,
    log_ref,
    key_ref,
    value_ref,
    dq_ref,
    dkey_ref,
    dvalue_ref,
    sum_ref,
):
    block, blocks = pl.program_id(0), pl.num_programs(0)
    rows = query_ref.shape[0]
    repeat = HEADS // KV_HEADS

    @pl.when(block == 0)
    def _():
        sum_ref[...] = jnp.zeros_like(sum_ref)

    allowed = allowed_pairs(first_ref, place_ref, rows, repeat)
    key_parts, value_parts = [], []
    for group in range(KV_HEADS):
        stacked = heads_stacked(query_ref, group, repeat)
        grads = heads_stacked(grad_ref, group, repeat)
        outs = heads_stacked(out_ref, group, repeat)
        inner = jnp.sum((grads.astype(jnp.float32) * outs).T, 0, keepdims=True)
        k = key_ref[:, group * HEAD_DIM : (group + 1) * HEAD_DIM]
        v = value_ref[:, group * HEAD_DIM : (group + 1) * HEAD_DIM]
        scores = times_transposed(k, stacked)
        shares = jnp.where(allowed, jnp.exp(scores - log_ref[group : group + 1, :]), 0.0)
        score_grads = (shares * (times_transposed(v, grads) - inner)).astype(jnp.bfloat16)
        value_parts.append(
            jnp.dot(shares.astype(jnp.bfloat16), grads, preferred_element_type=jnp.float32)
        )
        key_parts.append(jnp.dot(score_grads, stacked, preferred_element_type=jnp.float32))
        summed = sum_ref[group] + transposed_times(k, score_grads)
        sum_ref[group] = summed

        @pl.when(block == blocks - 1)
        def _():
            width = repeat * HEAD_DIM
            dq_ref[:, group * width : (group + 1) * width] = heads_beside(summed, repeat)

    dkey_ref[...] = jnp.concatenate(key_parts, 1).astype(dkey_ref.dtype)
    dvalue_ref[...] = jnp.concatenate(value_parts, 1).astype(dvalue_ref.dtype)


def whole_block(shape):
    return pl.BlockSpec(shape, lambda b: (0,) * len(shape))


def attention_forward(first_place, places, queries, all_keys, all_values):
    rows, width = queries.shape
    keys = block_span(all_keys.shape[0])
    kv_block = pl.BlockSpec((keys, all_keys.shape[1]), lambda b: (b, 0))
    columns = (HEADS // KV_HEADS) * rows
    return pl.pallas_call(
        forward_kernel,
        grid=(all_keys.shape[0] // keys,),
        in_specs=[
            pl.BlockSpec(memory_space=pltpu.SMEM),
            pl.BlockSpec((keys, 1), lambda b: (b, 0)),
            whole_block((rows, width)),
            kv_block,
            kv_block,
        ],
        out_specs=[whole_block((rows, width)), whole_block((KV_HEADS, columns))],
        out_shape=[
            jax.ShapeDtypeStruct((rows, width), jnp.float32),
            jax.ShapeDtypeStruct((KV_HEADS, columns), jnp.float32),
        ],
        scratch_shapes=[
            pltpu.VMEM((KV_HEADS, columns), jnp.float32),
            pltpu.VMEM((KV_HEADS, columns), jnp.float32),
            pltpu.VMEM((KV_HEADS, HEAD_DIM, columns), jnp.float32),
        ],
        compiler_params=pltpu.CompilerParams(vmem_limit_bytes=40 * 1024 * 1024),
        cost_estimate=pl.CostEstimate(
            flops=40 * all_keys.shape[0] * columns * HEAD_DIM,
            bytes_accessed=16 * 1024 * all_keys.shape[0],
            transcendentals=KV_HEADS * all_keys.shape[0] * columns,
        ),
    )(first_place, places, queries, all_keys, all_values)


def attention_backward(first_place, places, queries, grads, outs, logs, all_keys, all_values):
    rows, width = queries.shape
    keys = block_span(all_keys.shape[0])
    kv_block = pl.BlockSpec((keys, all_keys.shape[1]), lambda b: (b, 0))
    columns = (HEADS // KV_HEADS) * rows
    return pl.pallas_call(
        backward_kernel,
        grid=(all_keys.shape[0] // keys,),
        in_specs=[
            pl.BlockSpec(memory_space=pltpu.SMEM),
            pl.BlockSpec((keys, 1), lambda b: (b, 0)),
            whole_block((rows, width)),
            whole_block((rows, width)),
            whole_block((rows, width)),
            whole_block((KV_HEADS, columns)),
            kv_block,
            kv_block,
        ],
        out_specs=[
            whole_block((rows, width)),
            kv_block,
            kv_block,
        ],
        out_shape=[
            jax.ShapeDtypeStruct((rows, width), jnp.float32),
            jax.ShapeDtypeStruct(all_keys.shape, jnp.bfloat16),
            jax.ShapeDtypeStruct(all_keys.shape, jnp.bfloat16),
        ],
        scratch_shapes=[pltpu.VMEM((KV_HEADS, HEAD_DIM, columns), jnp.float32)],
        compiler_params=pltpu.CompilerParams(vmem_limit_bytes=40 * 1024 * 1024),
        cost_estimate=pl.CostEstimate(
            flops=40 * all_keys.shape[0] * columns * HEAD_DIM,
            bytes_accessed=16 * 1024 * all_keys.shape[0],
            transcendentals=KV_HEADS * all_keys.shape[0] * columns,
        ),
    )(first_place, places, queries, grads, outs, logs, all_keys, all_values)


def body(
    tokens, cotangent, norm_attn, w_query, w_key, w_value, w_out, norm_ffn, w_gate, w_up, w_down
):
    model_width = tokens.shape[2]
    kv_width = KV_HEADS * HEAD_DIM
    gains = core_gather(jnp.stack([norm_attn, norm_ffn]), 1)
    gain_attn, gain_ffn = gains[0], gains[1]
    joined_w = core_gather(jnp.concatenate([w_query, w_key, w_value], 1), 0)
    out_w = core_gather(w_out, 0)
    gate_w = lax.all_gather(w_gate, "fsdp", axis=0, tiled=True)
    up_w = lax.all_gather(w_up, "fsdp", axis=0, tiled=True)
    down_w = lax.all_gather(w_down, "fsdp", axis=0, tiled=True)
    gain_attn = gain_attn.astype(jnp.float32)
    gain_ffn = gain_ffn.astype(jnp.float32)
    local_rows = tokens.shape[1]
    groups = KV_HEADS
    repeat = HEADS // KV_HEADS
    kv_width = KV_HEADS * HEAD_DIM
    score_scale = HEAD_DIM ** (-0.5)
    first_pos = lax.axis_index("ctx") * local_rows
    inputs = tokens[0].astype(jnp.float32)
    grad_output = cotangent[0]
    attn_in, normed_one, factor_one = norm_forward(inputs, gain_attn)
    act_one = attn_in.astype(jnp.bfloat16)
    cosine_table, sine_table = rope_tables(first_pos, local_rows, HEAD_DIM)
    joined_pre = jnp.dot(act_one, joined_w, preferred_element_type=jnp.float32)
    query_pre = joined_pre[:, :model_width]
    key_pre = joined_pre[:, model_width : model_width + kv_width]
    value_pre = joined_pre[:, model_width + kv_width :]
    query_matrix = rotate(
        query_pre.reshape(local_rows, HEADS, HEAD_DIM), cosine_table, sine_table
    ).astype(jnp.bfloat16)
    query_matrix = query_matrix.reshape(local_rows, groups, repeat, HEAD_DIM)
    keys_here = rotate(
        key_pre.reshape(local_rows, groups, HEAD_DIM), cosine_table, sine_table
    ).astype(jnp.bfloat16)
    values_here = value_pre.reshape(local_rows, groups, HEAD_DIM).astype(jnp.bfloat16)
    key_order, value_order = gather_orders(lax.axis_size("ctx"))
    all_keys = gather_tree(keys_here.reshape(local_rows, kv_width), key_order)
    all_values = middle_swapped(
        gather_tree(values_here.reshape(local_rows, kv_width), value_order), value_order
    )
    places = slot_places(local_rows, key_order)
    scaled_queries = (
        query_matrix.reshape(local_rows, model_width) * jnp.bfloat16(score_scale)
    )
    first_place = first_pos.astype(jnp.int32).reshape(1)
    attended, log_totals = attention_forward(
        first_place, places, scaled_queries, all_keys, all_values
    )
    out_act = attended.reshape(local_rows, model_width).astype(jnp.bfloat16)
    residual = inputs + jnp.dot(out_act, out_w, preferred_element_type=jnp.float32)
    ffn_in, normed_two, factor_two = norm_forward(residual, gain_ffn)
    act_two = ffn_in.astype(jnp.bfloat16)
    gate_pre = jnp.dot(act_two, gate_w, preferred_element_type=jnp.float32)
    upward = jnp.dot(act_two, up_w, preferred_element_type=jnp.float32)
    silu_gate = jax.nn.silu(gate_pre)
    hidden = (silu_gate * upward).astype(jnp.bfloat16)
    result = (residual + jnp.dot(hidden, down_w, preferred_element_type=jnp.float32)).astype(
        jnp.bfloat16
    )
    grad_hidden = times_transposed(grad_output, down_w)
    grad_down_w = transposed_times(hidden, grad_output)
    sigmoid_gate = jax.nn.sigmoid(gate_pre)
    grad_gate = (
        grad_hidden * upward * sigmoid_gate * (1.0 + gate_pre * (1.0 - sigmoid_gate))
    ).astype(jnp.bfloat16)
    grad_upward = (grad_hidden * silu_gate).astype(jnp.bfloat16)
    grad_up_rest = transposed_times(act_two, grad_upward[:, 2 * grad_upward.shape[1] // 3 :])
    grad_act_two = times_transposed(grad_gate, gate_w) + times_transposed(grad_upward, up_w)
    back_two, grad_gain_ffn = norm_backward(grad_act_two, gain_ffn, normed_two, factor_two)
    grad_residual = grad_output.astype(jnp.float32) + back_two
    grad_attn = grad_residual.astype(jnp.bfloat16)
    grad_out_w = transposed_times(out_act, grad_attn)
    first_order, second_order, third_order = reduce_orders(lax.axis_size("ctx"))
    cut = 2 * grad_upward.shape[1] // 3
    wide = grad_gate.shape[1] + cut
    half_one = core_half(
        transposed_times(act_two, jnp.concatenate([grad_gate, grad_upward[:, :cut]], 1))
    )
    half_three = core_half(grad_down_w)
    grad_flat = times_transposed(grad_attn, out_w).astype(jnp.bfloat16)
    half_one, half_three, grad_flat = lax.optimization_barrier((half_one, half_three, grad_flat))
    grad_queries, partial_keys, partial_values = attention_backward(
        first_place, places, scaled_queries, grad_flat, attended, log_totals, all_keys, all_values
    )
    grad_queries = grad_queries * score_scale
    grad_keys = scatter_tree(partial_keys, key_order)
    grad_values = scatter_tree(middle_swapped(partial_values, value_order), value_order)
    grad_keys = grad_keys.reshape(local_rows, groups, HEAD_DIM)
    grad_query_pre = (
        unrotate(grad_queries.reshape(local_rows, HEADS, HEAD_DIM), cosine_table, sine_table)
        .reshape(local_rows, model_width)
        .astype(jnp.bfloat16)
    )
    grad_key_pre = (
        unrotate(grad_keys, cosine_table, sine_table)
        .reshape(local_rows, kv_width)
        .astype(jnp.bfloat16)
    )
    grad_value_pre = grad_values.reshape(local_rows, kv_width).astype(jnp.bfloat16)
    grad_query_w = transposed_times(act_one, grad_query_pre)
    grad_key_w = transposed_times(act_one, grad_key_pre)
    grad_value_w = transposed_times(act_one, grad_value_pre)
    grad_joined_pre = jnp.concatenate([grad_query_pre, grad_key_pre, grad_value_pre], 1)
    grad_act_one = times_transposed(grad_joined_pre, joined_w)
    back_one, grad_gain_attn = norm_backward(grad_act_one, gain_attn, normed_one, factor_one)
    grad_input = grad_residual + back_one
    gain_columns = jnp.stack([grad_gain_attn, grad_gain_ffn], 1)
    kept_parts = (grad_up_rest, grad_out_w, grad_key_w, grad_query_w, grad_value_w)
    spare = wide - sum(p.shape[1] for p in kept_parts)
    gain_columns = jnp.pad(gain_columns, ((0, 0), (0, max(spare, 2) - 2)))
    half_two = core_half(*kept_parts, gain_columns)
    shard_one = reduce_tree(half_one, first_order)
    shard_two = reduce_tree(half_two, second_order)
    shard_down = reduce_tree(half_three, third_order)
    ends = [0]
    for part in kept_parts:
        ends.append(ends[-1] + part.shape[1])
    up_rest, shard_out, shard_key, shard_query, shard_value = (
        shard_two[:, ends[i] : ends[i + 1]] for i in range(len(kept_parts))
    )
    shard_gate = shard_one[:, : grad_gate.shape[1]]
    shard_up = jnp.concatenate([shard_one[:, grad_gate.shape[1] :], up_rest], 1)
    shard_gains = shard_two[:, ends[-1] : ends[-1] + 2].T
    return (
        result[None],
        grad_input[None],
        shard_gains[0],
        shard_query,
        shard_key,
        shard_value,
        shard_out,
        shard_gains[1],
        shard_gate,
        shard_up,
        shard_down,
    )


def solution(mesh):
    placed = (
        P("fsdp", "ctx", None),
        P("fsdp", "ctx", None),
        P("fsdp"),
        P("fsdp", None),
        P("fsdp", None),
        P("fsdp", None),
        P("fsdp", None),
        P("fsdp"),
        P("fsdp", None),
        P("fsdp", None),
        P("fsdp", None),
    )
    return jax.shard_map(
        body,
        mesh=mesh,
        in_specs=placed,
        out_specs=(
            P("fsdp", "ctx", None),
            P("fsdp", "ctx", None),
            P("fsdp"),
            P("fsdp", None),
            P("fsdp", None),
            P("fsdp", None),
            P("fsdp", None),
            P("fsdp"),
            P("fsdp", None),
            P("fsdp", None),
            P("fsdp", None),
        ),
        check_vma=False,
    )
```

```python
import functools

import jax
import jax.numpy as jnp
from jax import lax
from jax.experimental import pallas as pl
from jax.experimental.pallas import tpu as pltpu
from jax.sharding import PartitionSpec as P

HEADS = 9
KV_HEADS = 3
HEAD_DIM = 64


norm_eps = 1e-05
rope_base = 10000.0
masked_score = -1e30


def rope_tables(first_pos, length, head_width):
    halfway = head_width // 2
    inverse = rope_base ** (-(jnp.arange(halfway, dtype=jnp.float32) * 2.0 / head_width))
    places = (first_pos + jnp.arange(length, dtype=jnp.int32)).astype(jnp.float32)
    angles = places[:, None] * inverse[None, :]
    return (jnp.cos(angles)[:, None, :], jnp.sin(angles)[:, None, :])


def rotate(values, cosine_table, sine_table):
    halfway = values.shape[-1] // 2
    former = values[..., :halfway]
    latter = values[..., halfway:]
    return jnp.concatenate(
        [former * cosine_table - latter * sine_table, latter * cosine_table + former * sine_table],
        -1,
    )


def unrotate(values, cosine_table, sine_table):
    halfway = values.shape[-1] // 2
    former = values[..., :halfway]
    latter = values[..., halfway:]
    return jnp.concatenate(
        [former * cosine_table + latter * sine_table, latter * cosine_table - former * sine_table],
        -1,
    )


def norm_forward(values, gain):
    factor = lax.rsqrt(jnp.mean(values * values, -1, keepdims=True) + norm_eps)
    normed = values * factor
    return (normed * gain, normed, factor)


def norm_backward(incoming, gain, normed, factor):
    scaled = incoming * gain
    back = factor * (scaled - normed * jnp.mean(scaled * normed, -1, keepdims=True))
    return (back, jnp.sum(incoming * normed, 0))


def times_transposed(left, right):
    return lax.dot_general(
        left, right, (((1,), (1,)), ((), ())), preferred_element_type=jnp.float32
    )


def transposed_times(left, right):
    return lax.dot_general(
        left, right, (((0,), (0,)), ((), ())), preferred_element_type=jnp.float32
    )


def block_span(count_rows):
    span_rows = count_rows
    while span_rows > 512 and span_rows % 2 == 0:
        span_rows = span_rows // 2
    return span_rows


def bit_count(devices):
    return devices.bit_length() - 1


def gather_orders(devices):
    order = list(range(bit_count(devices)))[::-1]
    return (order, order[:-2] + order[-2:][::-1])


def reduce_orders(devices):
    order = list(range(bit_count(devices)))
    return (order, order[:2][::-1] + order[2:], order[2:] + order[:2])


def swap(values, bit):
    count = lax.axis_size("ctx")
    return lax.ppermute(values, "ctx", [(i, i ^ (1 << bit)) for i in range(count)])


def own_bit(bit):
    return lax.rem(lax.axis_index("ctx") // (1 << bit), 2)


def gather_tree(block, order):
    held = block
    for bit in order:
        held = jnp.concatenate([held, swap(held, bit)], 0)
    return held


def scatter_tree(slots, order):
    held = slots.astype(jnp.float32)
    for bit in order[::-1]:
        half = held.shape[0] // 2
        held = held[:half] + swap(held[half:].astype(jnp.bfloat16), bit).astype(jnp.float32)
    return held


def middle_swapped(slots, order):
    if len(order) < 2:
        return slots
    part = slots.shape[0] // 4
    return jnp.concatenate(
        [slots[:part], slots[2 * part : 3 * part], slots[part : 2 * part], slots[3 * part :]], 0
    )


def slot_places(rows, order):
    slots = jnp.arange(1 << len(order), dtype=jnp.int32)
    flips = jnp.zeros_like(slots)
    for place, bit in enumerate(order):
        flips = flips + ((slots >> place) & 1) * (1 << bit)
    owners = flips ^ lax.axis_index("ctx").astype(jnp.int32)
    return (owners[:, None] * rows + jnp.arange(rows, dtype=jnp.int32)[None, :]).reshape(-1, 1)


def core_half(partial):
    own_index = lax.axis_index("fsdp")
    part_count = lax.axis_size("fsdp")
    rows = partial.shape[0] // part_count
    own = lax.dynamic_slice_in_dim(partial, own_index * rows, rows, 0)
    for shift in range(1, part_count):
        other = lax.rem(own_index + shift, part_count)
        sent = lax.dynamic_slice_in_dim(partial, other * rows, rows, 0).astype(jnp.bfloat16)
        moves = [(a, (a + shift) % part_count) for a in range(part_count)]
        own = own + lax.ppermute(sent, "fsdp", moves).astype(jnp.float32)
    return own


def reduce_tree(partial, order):
    held = partial
    path = []
    for bit in order:
        axis = 0 if held.shape[0] % 16 == 0 else 1
        half = held.shape[axis] // 2
        mine = own_bit(bit)
        kept = lax.dynamic_slice_in_dim(held, mine * half, half, axis)
        sent = lax.dynamic_slice_in_dim(held, (1 - mine) * half, half, axis)
        held = kept + swap(sent.astype(jnp.bfloat16), bit).astype(jnp.float32)
        path.append((bit, axis))
    held = held.astype(jnp.bfloat16)
    for bit, axis in path[::-1]:
        other = swap(held, bit)
        held = jnp.where(
            own_bit(bit) == 0,
            jnp.concatenate([held, other], axis),
            jnp.concatenate([other, held], axis),
        )
    return held.astype(jnp.float32)


def core_gather(block, axis):
    if lax.axis_size("fsdp") != 2:
        return lax.all_gather(block, "fsdp", axis=axis, tiled=True)
    other = lax.ppermute(block, "fsdp", [(0, 1), (1, 0)])
    return jnp.where(
        lax.axis_index("fsdp") == 0,
        jnp.concatenate([block, other], axis),
        jnp.concatenate([other, block], axis),
    )


def sum_tree(partial, order):
    held = partial
    for bit in order:
        held = held + swap(held, bit)
    count = lax.axis_size("fsdp")
    parts = held
    for shift in range(1, count):
        moves = [(a, (a + shift) % count) for a in range(count)]
        parts = parts + lax.ppermute(held, "fsdp", moves)
    held = parts
    return held


def heads_stacked(ref, group, repeat):
    first = group * repeat * HEAD_DIM
    return jnp.concatenate(
        [ref[:, first + r * HEAD_DIM : first + (r + 1) * HEAD_DIM] for r in range(repeat)], 0
    )


def heads_beside(transposed, repeat):
    rows = transposed.shape[1] // repeat
    back = transposed.T
    return jnp.concatenate([back[r * rows : (r + 1) * rows] for r in range(repeat)], 1)


def allowed_pairs(first_ref, place_ref, rows, repeat):
    query_place = lax.rem(lax.broadcasted_iota(jnp.int32, (1, repeat * rows), 1), rows)
    return place_ref[...] <= query_place + first_ref[0]


def forward_kernel(
    first_ref,
    place_ref,
    query_ref,
    key_ref,
    value_ref,
    out_ref,
    log_ref,
    high_ref,
    total_ref,
    sum_ref,
):
    block, blocks = pl.program_id(0), pl.num_programs(0)
    rows = query_ref.shape[0]
    repeat = HEADS // KV_HEADS

    @pl.when(block == 0)
    def _():
        high_ref[...] = jnp.full_like(high_ref, masked_score)
        total_ref[...] = jnp.zeros_like(total_ref)
        sum_ref[...] = jnp.zeros_like(sum_ref)

    allowed = allowed_pairs(first_ref, place_ref, rows, repeat)
    for group in range(KV_HEADS):
        stacked = heads_stacked(query_ref, group, repeat)
        k = key_ref[:, group * HEAD_DIM : (group + 1) * HEAD_DIM]
        v = value_ref[:, group * HEAD_DIM : (group + 1) * HEAD_DIM]
        scores = jnp.where(allowed, times_transposed(k, stacked), masked_score)
        old_high = high_ref[group : group + 1, :]
        new_high = jnp.maximum(old_high, jnp.max(scores, 0, keepdims=True))
        weights = jnp.exp(scores - new_high)
        keep = jnp.exp(old_high - new_high)
        total = total_ref[group : group + 1, :] * keep + jnp.sum(weights, 0, keepdims=True)
        summed = sum_ref[group] * keep + transposed_times(v, weights.astype(jnp.bfloat16))
        high_ref[group : group + 1, :] = new_high
        total_ref[group : group + 1, :] = total
        sum_ref[group] = summed

        @pl.when(block == blocks - 1)
        def _():
            log_ref[group : group + 1, :] = new_high + jnp.log(total)
            width = repeat * HEAD_DIM
            out_ref[:, group * width : (group + 1) * width] = heads_beside(summed / total, repeat)


def backward_kernel(
    first_ref,
    place_ref,
    query_ref,
    grad_ref,
    out_ref,
    log_ref,
    key_ref,
    value_ref,
    dq_ref,
    dkey_ref,
    dvalue_ref,
    sum_ref,
):
    block, blocks = pl.program_id(0), pl.num_programs(0)
    rows = query_ref.shape[0]
    repeat = HEADS // KV_HEADS

    @pl.when(block == 0)
    def _():
        sum_ref[...] = jnp.zeros_like(sum_ref)

    allowed = allowed_pairs(first_ref, place_ref, rows, repeat)
    key_parts, value_parts = [], []
    for group in range(KV_HEADS):
        stacked = heads_stacked(query_ref, group, repeat)
        grads = heads_stacked(grad_ref, group, repeat)
        outs = heads_stacked(out_ref, group, repeat)
        inner = jnp.sum((grads.astype(jnp.float32) * outs).T, 0, keepdims=True)
        k = key_ref[:, group * HEAD_DIM : (group + 1) * HEAD_DIM]
        v = value_ref[:, group * HEAD_DIM : (group + 1) * HEAD_DIM]
        scores = times_transposed(k, stacked)
        shares = jnp.where(allowed, jnp.exp(scores - log_ref[group : group + 1, :]), 0.0)
        score_grads = (shares * (times_transposed(v, grads) - inner)).astype(jnp.bfloat16)
        value_parts.append(
            jnp.dot(shares.astype(jnp.bfloat16), grads, preferred_element_type=jnp.float32)
        )
        key_parts.append(jnp.dot(score_grads, stacked, preferred_element_type=jnp.float32))
        summed = sum_ref[group] + transposed_times(k, score_grads)
        sum_ref[group] = summed

        @pl.when(block == blocks - 1)
        def _():
            width = repeat * HEAD_DIM
            dq_ref[:, group * width : (group + 1) * width] = heads_beside(summed, repeat)

    dkey_ref[...] = jnp.concatenate(key_parts, 1).astype(dkey_ref.dtype)
    dvalue_ref[...] = jnp.concatenate(value_parts, 1).astype(dvalue_ref.dtype)


def whole_block(shape):
    return pl.BlockSpec(shape, lambda b: (0,) * len(shape))


def attention_forward(first_place, places, queries, all_keys, all_values):
    rows, width = queries.shape
    keys = block_span(all_keys.shape[0])
    kv_block = pl.BlockSpec((keys, all_keys.shape[1]), lambda b: (b, 0))
    columns = (HEADS // KV_HEADS) * rows
    return pl.pallas_call(
        forward_kernel,
        grid=(all_keys.shape[0] // keys,),
        in_specs=[
            pl.BlockSpec(memory_space=pltpu.SMEM),
            pl.BlockSpec((keys, 1), lambda b: (b, 0)),
            whole_block((rows, width)),
            kv_block,
            kv_block,
        ],
        out_specs=[whole_block((rows, width)), whole_block((KV_HEADS, columns))],
        out_shape=[
            jax.ShapeDtypeStruct((rows, width), jnp.float32),
            jax.ShapeDtypeStruct((KV_HEADS, columns), jnp.float32),
        ],
        scratch_shapes=[
            pltpu.VMEM((KV_HEADS, columns), jnp.float32),
            pltpu.VMEM((KV_HEADS, columns), jnp.float32),
            pltpu.VMEM((KV_HEADS, HEAD_DIM, columns), jnp.float32),
        ],
        compiler_params=pltpu.CompilerParams(vmem_limit_bytes=40 * 1024 * 1024),
    )(first_place, places, queries, all_keys, all_values)


def attention_backward(first_place, places, queries, grads, outs, logs, all_keys, all_values):
    rows, width = queries.shape
    keys = block_span(all_keys.shape[0])
    kv_block = pl.BlockSpec((keys, all_keys.shape[1]), lambda b: (b, 0))
    columns = (HEADS // KV_HEADS) * rows
    return pl.pallas_call(
        backward_kernel,
        grid=(all_keys.shape[0] // keys,),
        in_specs=[
            pl.BlockSpec(memory_space=pltpu.SMEM),
            pl.BlockSpec((keys, 1), lambda b: (b, 0)),
            whole_block((rows, width)),
            whole_block((rows, width)),
            whole_block((rows, width)),
            whole_block((KV_HEADS, columns)),
            kv_block,
            kv_block,
        ],
        out_specs=[
            whole_block((rows, width)),
            kv_block,
            kv_block,
        ],
        out_shape=[
            jax.ShapeDtypeStruct((rows, width), jnp.float32),
            jax.ShapeDtypeStruct(all_keys.shape, jnp.bfloat16),
            jax.ShapeDtypeStruct(all_keys.shape, jnp.bfloat16),
        ],
        scratch_shapes=[pltpu.VMEM((KV_HEADS, HEAD_DIM, columns), jnp.float32)],
        compiler_params=pltpu.CompilerParams(vmem_limit_bytes=40 * 1024 * 1024),
    )(first_place, places, queries, grads, outs, logs, all_keys, all_values)


def body(
    tokens, cotangent, norm_attn, w_query, w_key, w_value, w_out, norm_ffn, w_gate, w_up, w_down
):
    model_width = tokens.shape[2]
    kv_width = KV_HEADS * HEAD_DIM
    gains = core_gather(jnp.stack([norm_attn, norm_ffn]), 1)
    gain_attn, gain_ffn = gains[0], gains[1]
    joined_w = core_gather(jnp.concatenate([w_query, w_key, w_value], 1), 0)
    out_w = core_gather(w_out, 0)
    gate_w = lax.all_gather(w_gate, "fsdp", axis=0, tiled=True)
    up_w = lax.all_gather(w_up, "fsdp", axis=0, tiled=True)
    down_w = lax.all_gather(w_down, "fsdp", axis=0, tiled=True)
    gain_attn = gain_attn.astype(jnp.float32)
    gain_ffn = gain_ffn.astype(jnp.float32)
    local_rows = tokens.shape[1]
    groups = KV_HEADS
    repeat = HEADS // KV_HEADS
    kv_width = KV_HEADS * HEAD_DIM
    score_scale = HEAD_DIM ** (-0.5)
    first_pos = lax.axis_index("ctx") * local_rows
    inputs = tokens[0].astype(jnp.float32)
    grad_output = cotangent[0]
    attn_in, normed_one, factor_one = norm_forward(inputs, gain_attn)
    act_one = attn_in.astype(jnp.bfloat16)
    cosine_table, sine_table = rope_tables(first_pos, local_rows, HEAD_DIM)
    joined_pre = jnp.dot(act_one, joined_w, preferred_element_type=jnp.float32)
    query_pre = joined_pre[:, :model_width]
    key_pre = joined_pre[:, model_width : model_width + kv_width]
    value_pre = joined_pre[:, model_width + kv_width :]
    query_matrix = rotate(
        query_pre.reshape(local_rows, HEADS, HEAD_DIM), cosine_table, sine_table
    ).astype(jnp.bfloat16)
    query_matrix = query_matrix.reshape(local_rows, groups, repeat, HEAD_DIM)
    keys_here = rotate(
        key_pre.reshape(local_rows, groups, HEAD_DIM), cosine_table, sine_table
    ).astype(jnp.bfloat16)
    values_here = value_pre.reshape(local_rows, groups, HEAD_DIM).astype(jnp.bfloat16)
    key_order, value_order = gather_orders(lax.axis_size("ctx"))
    all_keys = gather_tree(keys_here.reshape(local_rows, kv_width), key_order)
    all_values = middle_swapped(
        gather_tree(values_here.reshape(local_rows, kv_width), value_order), value_order
    )
    places = slot_places(local_rows, key_order)
    scaled_queries = (
        query_matrix.reshape(local_rows, model_width) * jnp.bfloat16(score_scale)
    )
    first_place = first_pos.astype(jnp.int32).reshape(1)
    attended, log_totals = attention_forward(
        first_place, places, scaled_queries, all_keys, all_values
    )
    out_act = attended.reshape(local_rows, model_width).astype(jnp.bfloat16)
    residual = inputs + jnp.dot(out_act, out_w, preferred_element_type=jnp.float32)
    ffn_in, normed_two, factor_two = norm_forward(residual, gain_ffn)
    act_two = ffn_in.astype(jnp.bfloat16)
    gate_pre = jnp.dot(act_two, gate_w, preferred_element_type=jnp.float32)
    upward = jnp.dot(act_two, up_w, preferred_element_type=jnp.float32)
    silu_gate = jax.nn.silu(gate_pre)
    hidden = (silu_gate * upward).astype(jnp.bfloat16)
    result = (residual + jnp.dot(hidden, down_w, preferred_element_type=jnp.float32)).astype(
        jnp.bfloat16
    )
    grad_hidden = times_transposed(grad_output, down_w)
    grad_down_w = transposed_times(hidden, grad_output)
    sigmoid_gate = jax.nn.sigmoid(gate_pre)
    grad_gate = (
        grad_hidden * upward * sigmoid_gate * (1.0 + gate_pre * (1.0 - sigmoid_gate))
    ).astype(jnp.bfloat16)
    grad_upward = (grad_hidden * silu_gate).astype(jnp.bfloat16)
    grad_gate_w = transposed_times(act_two, grad_gate)
    grad_up_w = transposed_times(act_two, grad_upward)
    grad_act_two = times_transposed(grad_gate, gate_w) + times_transposed(grad_upward, up_w)
    back_two, grad_gain_ffn = norm_backward(grad_act_two, gain_ffn, normed_two, factor_two)
    grad_residual = grad_output.astype(jnp.float32) + back_two
    grad_attn = grad_residual.astype(jnp.bfloat16)
    grad_out_w = transposed_times(out_act, grad_attn)
    first_order, second_order, third_order = reduce_orders(lax.axis_size("ctx"))
    shard_gate = reduce_tree(core_half(grad_gate_w), first_order)
    shard_up = reduce_tree(core_half(grad_up_w), second_order)
    shard_down = reduce_tree(core_half(grad_down_w), third_order)
    grad_flat = times_transposed(grad_attn, out_w).astype(jnp.bfloat16)
    grad_queries, partial_keys, partial_values = attention_backward(
        first_place, places, scaled_queries, grad_flat, attended, log_totals, all_keys, all_values
    )
    grad_queries = grad_queries * score_scale
    grad_keys = scatter_tree(partial_keys, key_order).reshape(local_rows, groups, HEAD_DIM)
    grad_values = scatter_tree(middle_swapped(partial_values, value_order), value_order)
    grad_query_pre = (
        unrotate(grad_queries.reshape(local_rows, HEADS, HEAD_DIM), cosine_table, sine_table)
        .reshape(local_rows, model_width)
        .astype(jnp.bfloat16)
    )
    grad_key_pre = (
        unrotate(grad_keys, cosine_table, sine_table)
        .reshape(local_rows, kv_width)
        .astype(jnp.bfloat16)
    )
    grad_value_pre = grad_values.reshape(local_rows, kv_width).astype(jnp.bfloat16)
    grad_query_w = transposed_times(act_one, grad_query_pre)
    grad_key_w = transposed_times(act_one, grad_key_pre)
    grad_value_w = transposed_times(act_one, grad_value_pre)
    grad_joined_pre = jnp.concatenate([grad_query_pre, grad_key_pre, grad_value_pre], 1)
    grad_act_one = times_transposed(grad_joined_pre, joined_w)
    back_one, grad_gain_attn = norm_backward(grad_act_one, gain_attn, normed_one, factor_one)
    grad_input = grad_residual + back_one
    shard_one = reduce_tree(
        core_half(jnp.concatenate([grad_out_w, grad_key_w], 1)), first_order
    )
    shard_two = reduce_tree(
        core_half(jnp.concatenate([grad_query_w, grad_value_w], 1)), second_order
    )
    shard_out, shard_key = shard_one[:, :model_width], shard_one[:, model_width:]
    shard_query, shard_value = shard_two[:, :model_width], shard_two[:, model_width:]
    gains = sum_tree(jnp.stack([grad_gain_attn, grad_gain_ffn]), first_order)
    shard_gains = lax.dynamic_slice_in_dim(
        gains, lax.axis_index("fsdp") * norm_attn.shape[0], norm_attn.shape[0], 1
    )
    return (
        result[None],
        grad_input[None],
        shard_gains[0],
        shard_query,
        shard_key,
        shard_value,
        shard_out,
        shard_gains[1],
        shard_gate,
        shard_up,
        shard_down,
    )


def solution(mesh):
    placed = (
        P("fsdp", "ctx", None),
        P("fsdp", "ctx", None),
        P("fsdp"),
        P("fsdp", None),
        P("fsdp", None),
        P("fsdp", None),
        P("fsdp", None),
        P("fsdp"),
        P("fsdp", None),
        P("fsdp", None),
        P("fsdp", None),
    )
    return jax.shard_map(
        body,
        mesh=mesh,
        in_specs=placed,
        out_specs=(
            P("fsdp", "ctx", None),
            P("fsdp", "ctx", None),
            P("fsdp"),
            P("fsdp", None),
            P("fsdp", None),
            P("fsdp", None),
            P("fsdp", None),
            P("fsdp"),
            P("fsdp", None),
            P("fsdp", None),
            P("fsdp", None),
        ),
        check_vma=False,
    )
```
